128 devices in a mesh: gx: 2 (over core), gy: 4 (over x), gz: 16 (over z, y).
Axes of the slice: x: 4, y: 4, z: 4, core: 2. Of those that a mesh axis runs over, the one named last changes fastest.
Arguments:
- jacobian: bfloat16 [4096, 7, 135, 135], P(('gx', 'gy', 'gz')), may hold values from -6 to 6
- prolong: bfloat16 [4096, 135, 135], P(('gx', 'gy', 'gz')), may hold values from -0.5 to 0.5
- residual: bfloat16 [4096, 135], P(('gx', 'gy', 'gz')), may hold values from -6 to 6
- neighbours: int32 [4096, 6], P(('gx', 'gy', 'gz')), may hold values from -1 to 4095, as said below
- agg_map: int32 [4096], P(('gx', 'gy', 'gz')), may hold values from 0 to 511, as said below
- owners: int32 [512], P(('gx', 'gy', 'gz')), may hold values from 0 to 12, as said below
Outputs:
- coarse: bfloat16 [2048, 7, 135, 135], P(('gx', 'gy', 'gz'))
- restricted: bfloat16 [2048, 135], P(('gx', 'gy', 'gz'))
The draws below stay inside these ranges and needn't reach their ends.
Inputs may be any that keep to these rules, and one draw needn't show every extreme that they name: `neighbours`: elements form a structured grid of bricks of 4 x 4 x 2 per device, laid out by the device's gx, gy, gz index; inside a device their numbering is an arbitrary permutation. The neighbour in direction -x or +x lies on the same device or on the device one step along gx (likewise y with gy, z with gz); exactly 8, 8 and 16 elements of a device have their x, y and z neighbour of one side off the device or absent. `agg_map`: aggregates are cubes of 2 x 2 x 2 elements of one device's brick; device d holds aggregates d * 4 to (d + 1) * 4 - 1. `owners`: owners are multiples of 4; each device hands exactly 1 of its aggregates to each such owner.
All inputs are finite; a program needn't handle non-finite values.
Results may differ from the reference program's by a relative error of at most 0.0051.
Values may be sent and summed in bfloat16 or wider, within the bound.
No kernel may reach another device: no remote copies, remote signals or barrier semaphores. Data moves between devices by JAX's collectives and lax.ppermute only.
A program may use at most 192 MiB of HBM per device.

```python
import jax
import jax.numpy as jnp
from jax import lax

B = 135
LX = 4
LY = 4
LZ = 2
E_DEV = 32
AGG_DEV = 4
SCAP = 1
ELEMS = 4096
CAPO = 16
N_GX = 2
N_GY = 4
N_GZ = 16


def cell_order(key):
    count = LX * LY * LZ
    devices = N_GX * N_GY * N_GZ
    keys = jax.random.split(jax.random.fold_in(key, 11), devices)
    return jax.vmap(lambda single: jax.random.permutation(single, count))(keys).astype(jnp.int32)


def cell_coords():
    count = LX * LY * LZ
    devices = N_GX * N_GY * N_GZ
    device = jnp.arange(devices, dtype=jnp.int32)[:, None]
    cell = jnp.arange(count, dtype=jnp.int32)[None, :]
    coord_x = device // (N_GY * N_GZ) * LX + cell // (LY * LZ)
    coord_y = device // N_GZ % N_GY * LY + cell // LZ % LY
    coord_z = device % N_GZ * LZ + cell % LZ
    return (coord_x, coord_y, coord_z)


def by_local(values, order):
    rows_index = jnp.arange(order.shape[0], dtype=jnp.int32)[:, None]
    return jnp.zeros(values.shape, jnp.int32).at[rows_index, order].set(values)


def draw_neighbours(key, part):
    count = LX * LY * LZ
    devices = N_GX * N_GY * N_GZ
    order = cell_order(key)
    coord_x, coord_y, coord_z = cell_coords()
    columns = []
    for step_x, step_y, step_z in ((-1, 0, 0), (1, 0, 0), (0, -1, 0), (0, 1, 0), (0, 0, -1), (0, 0, 1)):
        moved_x = coord_x + step_x
        moved_y = coord_y + step_y
        moved_z = coord_z + step_z
        inside = (moved_x >= 0) & (moved_x < LX * N_GX) & (moved_y >= 0) & (moved_y < LY * N_GY) & (moved_z >= 0) & (moved_z < LZ * N_GZ)
        moved_x = jnp.clip(moved_x, 0, LX * N_GX - 1)
        moved_y = jnp.clip(moved_y, 0, LY * N_GY - 1)
        moved_z = jnp.clip(moved_z, 0, LZ * N_GZ - 1)
        other_dev = (moved_x // LX * N_GY + moved_y // LY) * N_GZ + moved_z // LZ
        other_cell = (moved_x % LX * LY + moved_y % LY) * LZ + moved_z % LZ
        global_id = other_dev * count + order[other_dev, other_cell]
        columns.append(jnp.where(inside, global_id, -1))
    values = jnp.stack(columns, axis=-1).astype(jnp.int32)
    return by_local(values, order).reshape(devices * count, 6)


def draw_agg_map(key, part):
    count = LX * LY * LZ
    devices = N_GX * N_GY * N_GZ
    order = cell_order(key)
    coord_x, coord_y, coord_z = cell_coords()
    device = jnp.arange(devices, dtype=jnp.int32)[:, None]
    inner = (coord_x % LX // 2 * (LY // 2) + coord_y % LY // 2) * (LZ // 2) + coord_z % LZ // 2
    values = (device * (count // 8) + inner).astype(jnp.int32)
    return by_local(values, order).reshape(devices * count)


def draw_owners(key, part):
    devices = N_GX * N_GY * N_GZ
    keys = jax.random.split(jax.random.fold_in(key, 23), devices)
    listing = (jnp.arange(AGG_DEV, dtype=jnp.int32) // SCAP * (N_GZ // 4)).astype(jnp.int32)

    def single_device(single):
        return listing[jax.random.permutation(single, AGG_DEV)]
    return jax.vmap(single_device)(keys).reshape(-1).astype(jnp.int32)


def block_levels(key, shape, cuts, least, top_value):
    loudness, own = 1.0, jax.random.fold_in(key, 6)
    for dim, shards_of in cuts:
        draws = jnp.exp(jax.random.uniform(jax.random.fold_in(own, dim), (shards_of,), jnp.float32, least / len(cuts), top_value / len(cuts)))
        loudness = loudness * jnp.repeat(draws, shape[dim] // shards_of).reshape([-1 if axis == dim else 1 for axis in range(len(shape))])
    return loudness


def gaussian(key, shape, scale, reach, cuts=(), kind=jnp.bfloat16):
    array = scale * jax.random.normal(key, shape, jnp.float32)
    if cuts:
        array = array * block_levels(key, shape, cuts, -0.22, 0.18)
    return jnp.clip(array, -reach, reach).astype(kind)


def setup_inputs(seed: int = 0) -> dict:
    streams_of = jax.random.split(jax.random.key(seed), 7)
    return {
        "jacobian": gaussian(streams_of[0], (ELEMS, 7, B, B), 1.0, 6.0, ((0, 128),)),
        "prolong": gaussian(streams_of[1], (ELEMS, B, B), B ** -0.5, 0.5, ((0, 128),)),
        "residual": gaussian(streams_of[2], (ELEMS, B), 1.0, 6.0, ((0, 128),)),
        "neighbours": draw_neighbours(jax.random.fold_in(streams_of[6], 71), 0),
        "agg_map": draw_agg_map(jax.random.fold_in(streams_of[6], 71), 0),
        "owners": draw_owners(jax.random.fold_in(streams_of[6], 71), 0),
    }


def device_rows(device, jacobian, prolong, residual, neighbours, agg_map):
    first = (device * E_DEV).astype(jnp.int32)
    jac_dev = lax.dynamic_slice_in_dim(jacobian, first, E_DEV, 0)
    pro_dev = lax.dynamic_slice_in_dim(prolong, first, E_DEV, 0)
    res_dev = lax.dynamic_slice_in_dim(residual, first, E_DEV, 0)
    nbr_dev = lax.dynamic_slice_in_dim(neighbours, first, E_DEV, 0)
    agg_dev = lax.dynamic_slice_in_dim(agg_map, first, E_DEV, 0)
    is_valid = nbr_dev >= 0
    safe_ids = jnp.maximum(nbr_dev, 0)
    beside = jnp.where(is_valid[:, :, None, None], prolong[safe_ids], jnp.zeros((), jnp.bfloat16))
    gathered = jnp.concatenate([pro_dev[:, None], beside], axis=1)
    products = jnp.einsum("edij,edjk->edik", jac_dev.astype(jnp.float32), gathered.astype(jnp.float32)).astype(jnp.bfloat16)
    triple = jnp.einsum("eji,edjk->edik", pro_dev.astype(jnp.float32), products.astype(jnp.float32))
    same_agg = is_valid & (agg_map[safe_ids] == agg_dev[:, None])
    slot_ids = jnp.where(same_agg, 0, jnp.arange(1, 7, dtype=jnp.int32)[None, :])
    slot_ids = jnp.concatenate([jnp.zeros((E_DEV, 1), jnp.int32), slot_ids], axis=1)
    present = jnp.concatenate([jnp.ones((E_DEV, 1), bool), is_valid], axis=1)
    slot_hot = ((slot_ids[:, :, None] == jnp.arange(7, dtype=jnp.int32)) & present[:, :, None]).astype(jnp.float32)
    agg_hot = ((agg_dev - device * AGG_DEV)[:, None] == jnp.arange(AGG_DEV, dtype=jnp.int32)).astype(jnp.float32)
    coarse_rows = jnp.einsum("ea,eds,edik->asik", agg_hot, slot_hot, triple, precision=lax.Precision.HIGHEST)
    per_element = jnp.einsum("eji,ej->ei", pro_dev.astype(jnp.float32), res_dev.astype(jnp.float32))
    restr = jnp.dot(agg_hot.T, per_element, precision=lax.Precision.HIGHEST)
    return coarse_rows.astype(jnp.bfloat16), restr.astype(jnp.bfloat16)


def reference(jacobian, prolong, residual, neighbours, agg_map, owners):
    devices = N_GX * N_GY * N_GZ
    rows_all, restr_all = lax.map(lambda device: device_rows(device, jacobian, prolong, residual, neighbours, agg_map), jnp.arange(devices, dtype=jnp.int32))
    rows_all = rows_all.reshape(devices * AGG_DEV, 7, B, B)
    restr_all = restr_all.reshape(devices * AGG_DEV, B)
    owner_dev = owners.reshape(devices, AGG_DEV)
    counter = jnp.arange(AGG_DEV, dtype=jnp.int32)
    earlier = (owner_dev[:, None, :] == owner_dev[:, :, None]) & (counter[None, None, :] < counter[None, :, None])
    within = jnp.sum(earlier.astype(jnp.int32), axis=-1).reshape(-1)
    source = jnp.arange(devices * AGG_DEV, dtype=jnp.int32) // AGG_DEV
    target = (source // N_GZ) * N_GZ + owners
    row_ids = target * CAPO + (source % N_GZ) * SCAP + within
    coarse = jnp.zeros((devices * CAPO, 7, B, B), jnp.bfloat16).at[row_ids].set(rows_all)
    restricted = jnp.zeros((devices * CAPO, B), jnp.bfloat16).at[row_ids].set(restr_all)
    return coarse, restricted
```

```python
import functools

import jax
import jax.numpy as jnp
from jax import lax
from jax.experimental import pallas as pl
from jax.experimental.pallas import tpu as pltpu
from jax.sharding import Mesh, PartitionSpec as P

E = 32
W = 135
H = 136
L = 128
R = W - L
BF = jnp.bfloat16
F32 = jnp.float32
VMEM_LIMIT = 56 * 1024 * 1024


def smem():
    return pl.BlockSpec(memory_space=pltpu.SMEM)


def vmem():
    return pl.BlockSpec(memory_space=pltpu.VMEM)


def spread(block, main, rest):
    def step(i, carry):
        for u in range(5):
            row = i * 5 + u
            values = block(row).astype(F32)
            at = pl.ds(pl.multiple_of(row * E, E), E)
            main[at, :] = values[:, :L]
            rest[at, 0:R] = values[:, L:]
        return carry

    lax.fori_loop(0, W // 5, step, 0)


def clear(main, rest):
    main[W * E : H * E, :] = jnp.zeros((E, L), F32)
    rest[...] = jnp.zeros((H * E, L), F32)


def take(ref, element):
    return ref[pl.ds(element, H, stride=E), :]


def pack_kernel(scal, nbr, agg, own, p_ref, meta, pz, xs, ys, pt, main, rest):
    base = scal[0]

    def place(e, carry):
        def near(direction):
            local = nbr[direction, e] - base
            here = (local >= 0) & (local < E)
            safe = jnp.clip(local, 0, E - 1)
            same = here & (agg[safe] == agg[e])
            return here.astype(jnp.int32), same.astype(jnp.int32)

        here_xm, odd_x = near(0)
        here_xp, _ = near(1)
        here_ym, odd_y = near(2)
        here_yp, _ = near(3)
        _, odd_z = near(4)
        agg_x = jnp.where(odd_x == 1, 1 - here_xp, here_xm)
        agg_y = jnp.where(odd_y == 1, 1 - here_yp, here_ym)
        meta[odd_z * 16 + (2 * agg_x + odd_x) * 4 + 2 * agg_y + odd_y] = e
        owner = own[agg[e] - scal[1]]
        meta[E + agg_x * 2 + agg_y] = lax.rem(owner // 4 - scal[2] + 4, 4)
        return carry

    lax.fori_loop(0, E, place, 0)
    clear(main, rest)
    spread(lambda row: p_ref[row], main, rest)
    for oz in range(2):
        plane = jnp.zeros((H, L), F32)
        for xy in range(16):
            e = meta[oz * 16 + xy]
            a = take(main, e)
            b = take(rest, e)
            pz[oz, xy] = a.astype(BF)
            plane = plane + (pltpu.roll(b, R * xy, 1) if xy else b)
            pt[oz * 16 + xy] = jnp.concatenate([a.T, b.T[:8]], axis=0).astype(BF)
        pz[oz, 16] = plane.astype(BF)
    face = jnp.where(scal[3] == 0, 12, 0)
    for oz in range(2):
        for v in range(4):
            xs[oz * 4 + v] = pz[oz, face + v]
            ys[0, oz * 4 + v] = pz[oz, v * 4]
            ys[1, oz * 4 + v] = pz[oz, v * 4 + 3]
        xs[8 + oz] = pz[oz, 16]
        ys[0, 8 + oz] = pz[oz, 16]
        ys[1, 8 + oz] = pz[oz, 16]


def pair_kernel(axis, scal, meta, jac, pz, ghost_m, ghost_p, pt, *rest_refs):
    first = axis == 0
    last = axis == 2
    if first:
        res_t, rows, carry_out, rem_out, main, rest, x0, xs, keep = rest_refs
    elif last:
        carry_in, rem_in, rows, main, rest, x0, xs = rest_refs
    else:
        carry_in, rem_in, rows, carry_out, rem_out, main, rest, x0, xs = rest_refs
    step = pl.program_id(0)
    lane = lax.broadcasted_iota(jnp.int32, (H, L), 1)

    @pl.when(step == 0)
    def _():
        clear(main, rest)

    spread(lambda row: jac[0, row], main, rest)

    def product(c, plane_main, plane_rest, idx):
        e = meta[c]
        left = jnp.concatenate([take(main, e), take(rest, e)[:, :8]], axis=1).astype(BF)
        right = jnp.concatenate([plane_main, plane_rest], axis=1)
        out = jnp.dot(left, right, preferred_element_type=F32)
        low = R * idx
        good = (lane >= low) & (lane < low + R)
        return jnp.concatenate([out[:, :L], jnp.where(good, out[:, L:], 0.0)], axis=1)

    def where_is(q, octant):
        ax, ay = q // 2, lax.rem(q, 2)
        ox, oy, oz = octant // 4, octant // 2 % 2, octant % 2
        return 2 * ax + ox, 2 * ay + oy, oz

    def direct(q, carry):
        for octant in range(8):
            x, y, oz = where_is(q, octant)
            idx = x * 4 + y
            keep[q * 8 + octant] = product(oz * 16 + idx, pz[oz, idx], pz[oz, 16], idx)
        return carry

    def sided(minus):
        def run(q, carry):
            for octant in range(8):
                bit = (octant // 4, octant // 2 % 2, octant % 2)[axis]
                x, y, oz = where_is(q, octant)
                c = oz * 16 + x * 4 + y
                if (bit == 1) == minus:
                    shift = -1 if minus else 1
                    nx, ny, nz = x, y, oz
                    if axis == 0:
                        nx = x + shift
                    elif axis == 1:
                        ny = y + shift
                    else:
                        nz = oz + shift
                    idx = nx * 4 + ny
                    out = product(c, pz[nz, idx], pz[nz, 16], idx)
                    if first:
                        out = out + keep[q * 8 + octant]
                        low = L + 112
                        e = meta[c]
                        column = pltpu.roll(res_t[...], lax.rem(112 - e + L, L), 1)
                        out = jnp.concatenate(
                            [out[:, :L], jnp.where(lane == 112, column, out[:, L:])], axis=1
                        )
                    x0[q * 8 + octant] = out.astype(BF)
                    continue
                ghost = ghost_m if minus else ghost_p
                if axis == 2:
                    idx = x * 4 + y
                    out = product(c, ghost[idx], ghost[16], idx)
                else:
                    along, other = (x, y) if axis == 0 else (y, x)
                    spot = along + (-1 if minus else 1)
                    outside = (spot < 0) | (spot > 3)
                    spot = lax.rem(spot + 4, 4)
                    idx = spot * 4 + other if axis == 0 else other * 4 + spot
                    plane_main = jnp.where(outside, ghost[oz * 4 + other], pz[oz, idx])
                    plane_rest = jnp.where(outside, ghost[8 + oz], pz[oz, 16])
                    out = product(c, plane_main, plane_rest, idx)
                    if axis == 0:
                        absent = outside & (scal[3] == (0 if minus else 1))
                        out = out * jnp.where(absent, 0.0, 1.0)
                xs[q * 8 + octant] = out.astype(BF)
            return carry

        return run

    offset = 1 if first else 0
    if first:

        @pl.when(step == 0)
        def _():
            lax.fori_loop(0, 4, direct, 0)

    @pl.when(step == offset)
    def _():
        lax.fori_loop(0, 4, sided(True), 0)

    @pl.when(step == offset + 1)
    def _():
        lax.fori_loop(0, 4, sided(False), 0)

        def finish(q, carry):
            ax, ay = q // 2, lax.rem(q, 2)
            at = meta[E + q]

            def gather(ref, octants):
                acc = None
                for octant in octants:
                    x, y, oz = where_is(q, octant)
                    part = jnp.dot(
                        pt[oz * 16 + x * 4 + y], ref[q * 8 + octant], preferred_element_type=F32
                    )
                    acc = part if acc is None else acc + part
                return acc

            def fold(raw, spots, slot):
                total = None
                for spot in spots:
                    turned = pltpu.roll(raw, lax.rem(R * slot - R * spot + 2 * L, L), 1)
                    total = turned if total is None else total + turned
                good = (lane >= R * slot) & (lane < R * slot + R)
                return jnp.where(good, total, 0.0)

            acc0 = gather(x0, range(8))
            remainder = jnp.zeros((H, L), F32)
            for side in range(2):
                slot = 1 + 2 * axis + side
                chosen = [o for o in range(8) if (o // 4, o // 2 % 2, o % 2)[axis] == side]
                acc = gather(xs, chosen)
                rows[at, side] = acc[:, :L].astype(BF)
                if axis == 0:
                    nx = lax.rem(2 * ax + (-1 if side == 0 else 2) + 4, 4)
                    spots = [nx * 4 + 2 * ay + v for v in range(2)]
                elif axis == 1:
                    ny = lax.rem(2 * ay + (-1 if side == 0 else 2) + 4, 4)
                    spots = [(2 * ax + v) * 4 + ny for v in range(2)]
                else:
                    spots = [(2 * ax + v // 2) * 4 + 2 * ay + v % 2 for v in range(4)]
                remainder = remainder + fold(acc[:, L:], spots, slot)
            if not first:
                acc0 = acc0 + carry_in[at]
                remainder = remainder + rem_in[at]
            if not last:
                carry_out[at] = acc0
                rem_out[at] = remainder
            else:
                rows[at, 2] = acc0[:, :L].astype(BF)
                spots = [(2 * ax + v // 2) * 4 + 2 * ay + v % 2 for v in range(4)]
                raw = acc0[:, L:]
                remainder = remainder + fold(raw, spots, 0)
                moved = pltpu.roll(raw, 49 - 112 + L, 1)
                remainder = jnp.where(lane == 49, moved, remainder)
                rows[at, 3] = remainder.astype(BF)
            return carry

        lax.fori_loop(0, 4, finish, 0)


def pair_call(axis, scal, meta, jac, pz, ghost_m, ghost_p, pt, extra):
    first, last = axis == 0, axis == 2
    steps = 3 if first else 2
    start = 0 if first else 1 + 2 * axis
    planes = 4 if last else 2
    out_shape = [jax.ShapeDtypeStruct((4, planes, H, L), BF)]
    if not last:
        out_shape.append(jax.ShapeDtypeStruct((4, H, 2 * L), F32))
        out_shape.append(jax.ShapeDtypeStruct((4, H, L), F32))
    scratch = [
        pltpu.VMEM((H * E, L), F32),
        pltpu.VMEM((H * E, L), F32),
        pltpu.VMEM((E, H, 2 * L), BF),
        pltpu.VMEM((E, H, 2 * L), BF),
    ]
    if first:
        scratch.append(pltpu.VMEM((E, H, 2 * L), F32))
    operands = (scal, meta, jac, pz, ghost_m, ghost_p, pt) + extra
    in_specs = [smem(), smem(), pl.BlockSpec((1, W, E, W), lambda s: (start + s, 0, 0, 0))]
    in_specs += [vmem()] * (len(operands) - 3)
    return pl.pallas_call(
        functools.partial(pair_kernel, axis),
        grid=(steps,),
        in_specs=in_specs,
        out_specs=[vmem()] * len(out_shape),
        out_shape=out_shape,
        scratch_shapes=scratch,
        compiler_params=pltpu.CompilerParams(vmem_limit_bytes=VMEM_LIMIT),
        cost_estimate=pl.CostEstimate(
            flops=6_000_000_000, bytes_accessed=8_000_000, transcendentals=0
        ),
        name="pair_" + "xyz"[axis],
    )(*operands)


def final_kernel(scal, *refs):
    parts = [refs[6 * p : 6 * p + 6] for p in range(3)]
    coarse, restricted, s1, s2 = refs[18:]
    step = pl.program_id(0)
    lane = lax.broadcasted_iota(jnp.int32, (H, L), 1)
    layout = [
        [(0, 0), (0, 1), (1, 0), (1, 1)],
        [(2, 0), (2, 1), (4, 0), (4, 1)],
        [(4, 2), (4, 3), (5, 2), (5, 3)],
        [(5, 0), (5, 1), (3, 0), (3, 1)],
    ]

    def slot_of(y, d):
        return lax.rem(scal[2] - d + 4, 4) * 4 + y

    def fill(part, plane, dest, columns):
        acc = jnp.zeros((H, L), F32)
        for y in range(4):
            for d in range(4):
                which, row = layout[y][d]
                slot = slot_of(y, d)
                value = parts[part][which][row, plane].astype(F32)
                dest[pl.ds(slot, H, stride=16), :] = value
                if columns:
                    turned = pltpu.roll(value, lax.rem(slot - 49 + L, L), 1)
                    acc = jnp.where(lane == slot, turned, acc)
        return acc

    @pl.when(scal[4] == 0)
    def _():
        coarse[...] = jnp.zeros_like(coarse)
        restricted[...] = jnp.zeros_like(restricted)

    @pl.when(scal[4] == 1)
    def _():
        @pl.when(step == 0)
        def _():
            acc = fill(2, 3, s2, True)
            restricted[...] = acc.T[:16, :W].astype(BF)

        sources = [(2, 2), (0, 0), (0, 1), (1, 0), (1, 1), (2, 0), (2, 1)]
        for k in range(7):

            @pl.when(step == k)
            def _():
                fill(*sources[k], s1, False)

        turn = lax.rem(L - R * step, L)

        def write(i, carry):
            for u in range(5):
                row = i * 5 + u
                at = pl.ds(pl.multiple_of(row * 16, 16), 16)
                tail = pltpu.roll(s2[at, :], turn, 1)
                coarse[0, row] = jnp.concatenate([s1[at, :], tail[:, :R]], axis=1).astype(BF)
            return carry

        lax.fori_loop(0, W // 5, write, 0)


def final_call(scal, parts):
    operands = [scal] + [a for part in parts for a in part]
    return pl.pallas_call(
        final_kernel,
        grid=(7,),
        in_specs=[smem()] + [vmem()] * 18,
        out_specs=[pl.BlockSpec((1, W, 16, W), lambda s: (s, 0, 0, 0)), vmem()],
        out_shape=[jax.ShapeDtypeStruct((7, W, 16, W), BF), jax.ShapeDtypeStruct((16, W), BF)],
        scratch_shapes=[pltpu.VMEM((H * 16, L), F32), pltpu.VMEM((H * 16, L), F32)],
        compiler_params=pltpu.CompilerParams(vmem_limit_bytes=VMEM_LIMIT),
        name="assemble",
    )(*operands)


def ship(rows):
    near = [rows[0]]
    for d in range(1, 4):
        near.append(lax.ppermute(rows[d], "zz", [(i, (i + d) % 4) for i in range(4)]))
    low = jnp.stack(near[:2])
    high = jnp.stack(near[2:])
    down = lax.ppermute(low, "yy", [(1, 0), (2, 1)])
    up = lax.ppermute(high, "yy", [(3, 0), (2, 3)])
    down2 = lax.ppermute(jnp.concatenate([high, down]), "yy", [(1, 0)])
    up2 = lax.ppermute(jnp.concatenate([low, up]), "yy", [(3, 0)])
    return low, high, down, up, down2, up2


def body(jacobian, prolong, residual, neighbours, agg_map, owners):
    gx, gy = lax.axis_index("gx"), lax.axis_index("gy")
    zz, yy = lax.axis_index("zz"), lax.axis_index("yy")
    device = (gx * 4 + gy) * 16 + zz * 4 + yy
    scal = jnp.stack(
        [device * E, device * 4, zz, gx, (yy == 0).astype(jnp.int32)]
    ).astype(jnp.int32)
    jac = jnp.transpose(jacobian, (1, 2, 0, 3))
    pro = jnp.transpose(prolong, (1, 0, 2))
    res_t = jnp.pad(residual.T.astype(F32), ((0, 1), (0, L - E)))
    meta, pz, xs, ys, pt = pl.pallas_call(
        pack_kernel,
        in_specs=[smem()] * 4 + [vmem()],
        out_specs=[smem()] + [vmem()] * 4,
        out_shape=[
            jax.ShapeDtypeStruct((40,), jnp.int32),
            jax.ShapeDtypeStruct((2, 17, H, L), BF),
            jax.ShapeDtypeStruct((10, H, L), BF),
            jax.ShapeDtypeStruct((2, 10, H, L), BF),
            jax.ShapeDtypeStruct((E, H, H), BF),
        ],
        scratch_shapes=[pltpu.VMEM((H * E, L), F32), pltpu.VMEM((H * E, L), F32)],
        compiler_params=pltpu.CompilerParams(vmem_limit_bytes=VMEM_LIMIT),
        name="pack",
    )(scal, neighbours.T, agg_map, owners, pro)
    gz = ("zz", "yy")
    ghost_x = lax.ppermute(xs, "gx", [(0, 1), (1, 0)])
    ghost_zm = lax.ppermute(pz[1], gz, [(i, i + 1) for i in range(15)])
    ghost_zp = lax.ppermute(pz[0], gz, [(i + 1, i) for i in range(15)])
    ghost_ym = lax.ppermute(ys[1], "gy", [(i, i + 1) for i in range(3)])
    ghost_yp = lax.ppermute(ys[0], "gy", [(i + 1, i) for i in range(3)])
    rows_x, carry, rem = pair_call(0, scal, meta, jac, pz, ghost_x, ghost_x, pt, (res_t,))
    part_x = ship(rows_x)
    rows_y, carry, rem = pair_call(1, scal, meta, jac, pz, ghost_ym, ghost_yp, pt, (carry, rem))
    part_y = ship(rows_y)
    (rows_z,) = pair_call(2, scal, meta, jac, pz, ghost_zm, ghost_zp, pt, (carry, rem))
    part_z = ship(rows_z)
    coarse, restricted = final_call(scal, (part_x, part_y, part_z))
    return jnp.transpose(coarse, (2, 0, 1, 3)), restricted


def solution(mesh):
    fine = Mesh(mesh.devices.reshape(2, 4, 4, 4), ("gx", "gy", "zz", "yy"))
    every = ("gx", "gy", "zz", "yy")
    return jax.shard_map(
        body,
        mesh=fine,
        in_specs=(P(every), P(every), P(every), P(every), P(every), P(every)),
        out_specs=(P(every), P(every)),
        check_vma=False,
    )
```

```python
import functools

import jax
import jax.numpy as jnp
from jax import lax
from jax.experimental import pallas as pl
from jax.experimental.pallas import tpu as pltpu
from jax.sharding import Mesh, PartitionSpec as P

E = 32
W = 135
H = 136
L = 128
R = W - L
PE = 36
PS = 20
BF = jnp.bfloat16
F32 = jnp.float32
VMEM_LIMIT = 56 * 1024 * 1024


def smem():
    return pl.BlockSpec(memory_space=pltpu.SMEM)


def vmem():
    return pl.BlockSpec(memory_space=pltpu.VMEM)


def spread(block, main, rest):
    def step(i, carry):
        for u in range(5):
            row = i * 5 + u
            values = block(row).astype(F32)
            at = pl.ds(row * PE, E)
            main[at, :] = values[:, :L]
            rest[at, 0:R] = values[:, L:]
        return carry

    lax.fori_loop(0, W // 5, step, 0)


def clear(main, rest):
    main[W * PE : H * PE, :] = jnp.zeros((PE, L), F32)
    rest[...] = jnp.zeros((H * PE, L), F32)


def take(ref, element):
    return ref[pl.ds(element, H, stride=PE), :]


def pack_kernel(scal, nbr, agg, own, p_ref, meta, pz0, pz1, xs, ys0, ys1, pt, main, rest):
    pz, ys = (pz0, pz1), (ys0, ys1)
    base = scal[0]

    def place(e, carry):
        def near(direction):
            local = nbr[direction, e] - base
            here = (local >= 0) & (local < E)
            safe = jnp.clip(local, 0, E - 1)
            same = here & (agg[safe] == agg[e])
            return here.astype(jnp.int32), same.astype(jnp.int32)

        here_xm, odd_x = near(0)
        here_xp, _ = near(1)
        here_ym, odd_y = near(2)
        here_yp, _ = near(3)
        _, odd_z = near(4)
        agg_x = jnp.where(odd_x == 1, 1 - here_xp, here_xm)
        agg_y = jnp.where(odd_y == 1, 1 - here_yp, here_ym)
        meta[odd_z * 16 + (2 * agg_x + odd_x) * 4 + 2 * agg_y + odd_y] = e
        owner = own[agg[e] - scal[1]]
        meta[E + agg_x * 2 + agg_y] = owner // 4
        return carry

    lax.fori_loop(0, E, place, 0)
    clear(main, rest)
    spread(lambda row: p_ref[row], main, rest)
    for oz in range(2):
        plane = jnp.zeros((H, L), F32)
        for xy in range(16):
            e = meta[oz * 16 + xy]
            a = take(main, e)
            b = take(rest, e)
            pz[oz][xy] = a.astype(BF)
            plane = plane + (pltpu.roll(b, R * xy, 1) if xy else b)
            pt[oz * 16 + xy] = jnp.concatenate([a.T, b.T[:8]], axis=0).astype(BF)
        pz[oz][16] = plane.astype(BF)
    face = jnp.where(scal[3] == 0, 12, 0)
    for oz in range(2):
        for v in range(4):
            xs[oz * 4 + v] = pz[oz][face + v]
            ys[0][oz * 4 + v] = pz[oz][v * 4]
            ys[1][oz * 4 + v] = pz[oz][v * 4 + 3]
        xs[8 + oz] = pz[oz][16]
        ys[0][8 + oz] = pz[oz][16]
        ys[1][8 + oz] = pz[oz][16]


def pack_call(*operands):
    return pl.pallas_call(
        pack_kernel,
        in_specs=[smem()] * 4 + [vmem()],
        out_specs=[smem()] + [vmem()] * 6,
        out_shape=[
            jax.ShapeDtypeStruct((40,), jnp.int32),
            jax.ShapeDtypeStruct((17, H, L), BF),
            jax.ShapeDtypeStruct((17, H, L), BF),
            jax.ShapeDtypeStruct((10, H, L), BF),
            jax.ShapeDtypeStruct((10, H, L), BF),
            jax.ShapeDtypeStruct((10, H, L), BF),
            jax.ShapeDtypeStruct((E, H, H), BF),
        ],
        scratch_shapes=[pltpu.VMEM((H * PE, L), F32), pltpu.VMEM((H * PE, L), F32)],
        compiler_params=pltpu.CompilerParams(vmem_limit_bytes=VMEM_LIMIT),
        name="pack",
    )(*operands)


def block_kernel(kinds, scal, meta, jac, pz, ghosts, pt, res_t, rem_in, rows, rem_out, scratch):
    main, rest, x0, xs, keep = scratch
    step = pl.program_id(0)
    lane = lax.broadcasted_iota(jnp.int32, (H, L), 1)

    @pl.when(step == 0)
    def _():
        clear(main, rest)

    spread(lambda row: jac[0, row], main, rest)

    def product(c, plane_main, plane_rest, idx):
        e = meta[c]
        left = jnp.concatenate([take(main, e), take(rest, e)[:, :8]], axis=1).astype(BF)
        right = jnp.concatenate([plane_main, plane_rest], axis=1)
        out = jnp.dot(left, right, preferred_element_type=F32)
        low = R * idx
        good = (lane >= low) & (lane < low + R)
        return jnp.concatenate([out[:, :L], jnp.where(good, out[:, L:], 0.0)], axis=1)

    def where_is(q, octant):
        ax, ay = q // 2, lax.rem(q, 2)
        ox, oy, oz = octant // 4, octant // 2 % 2, octant % 2
        return 2 * ax + ox, 2 * ay + oy, oz

    def bits(octant):
        return octant // 4, octant // 2 % 2, octant % 2

    def direct(q):
        for octant in range(8):
            x, y, oz = where_is(q, octant)
            idx = x * 4 + y
            keep[q * 8 + octant] = product(oz * 16 + idx, pz[oz][idx], pz[oz][16], idx)

    def same(k, q):
        axis, shift = (k - 1) // 2, -1 if k % 2 else 1
        for octant in range(8):
            if bits(octant)[axis] != (1 if shift < 0 else 0):
                continue
            x, y, oz = where_is(q, octant)
            near = [x, y, oz]
            near[axis] = near[axis] + shift
            idx = near[0] * 4 + near[1]
            out = product(oz * 16 + x * 4 + y, pz[near[2]][idx], pz[near[2]][16], idx)
            out = out + keep[q * 8 + octant]
            if axis < 2:
                keep[q * 8 + octant] = out
            else:
                e = meta[oz * 16 + x * 4 + y]
                column = pltpu.roll(res_t[...], lax.rem(112 - e + L, L), 1)
                out = jnp.concatenate([out[:, :L], jnp.where(lane == 112, column, out[:, L:])], axis=1)
                x0[q * 8 + octant] = out.astype(BF)

    def outside(k, q):
        axis, shift = (k - 1) // 2, -1 if k % 2 else 1
        ghost = ghosts[k]
        for octant in range(8):
            if bits(octant)[axis] != (0 if shift < 0 else 1):
                continue
            x, y, oz = where_is(q, octant)
            c = oz * 16 + x * 4 + y
            if axis == 2:
                idx = x * 4 + y
                out = product(c, ghost[idx], ghost[16], idx)
                edge = 0 if shift < 0 else 15
                absent = scal[2] * 4 + scal[6] == edge
            else:
                along, other = (x, y) if axis == 0 else (y, x)
                spot = along + shift
                off = (spot < 0) | (spot > 3)
                spot = lax.rem(spot + 4, 4)
                idx = spot * 4 + other if axis == 0 else other * 4 + spot
                plane_main = jnp.where(off, ghost[oz * 4 + other], pz[oz][idx])
                plane_rest = jnp.where(off, ghost[8 + oz], pz[oz][16])
                out = product(c, plane_main, plane_rest, idx)
                edge = 0 if shift < 0 else (1, 3)[axis]
                absent = off & (scal[(3, 5)[axis]] == edge)
            xs[q * 8 + octant] = (out * jnp.where(absent, 0.0, 1.0)).astype(BF)

    def gather(ref, q, octants):
        acc = None
        for octant in octants:
            x, y, oz = where_is(q, octant)
            part = jnp.dot(pt[oz * 16 + x * 4 + y], ref[q * 8 + octant], preferred_element_type=F32)
            acc = part if acc is None else acc + part
        return acc

    def fold(raw, spots, slot):
        total = None
        for spot in spots:
            turned = pltpu.roll(raw, lax.rem(R * slot - R * spot + 2 * L, L), 1)
            total = turned if total is None else total + turned
        good = (lane >= R * slot) & (lane < R * slot + R)
        return jnp.where(good, total, 0.0)

    def finish_sides(axis, q):
        ax, ay = q // 2, lax.rem(q, 2)
        at = meta[E + q]
        remainder = (rem_out if axis == 1 else rem_in)[at]
        for side in range(2):
            acc = gather(xs, q, [o for o in range(8) if bits(o)[axis] == side])
            rows[at, 2 * (axis % 2) + side] = acc[:, :L].astype(BF)
            if axis == 0:
                nx = lax.rem(2 * ax + (-1 if side == 0 else 2) + 4, 4)
                spots = [nx * 4 + 2 * ay + v for v in range(2)]
            elif axis == 1:
                ny = lax.rem(2 * ay + (-1 if side == 0 else 2) + 4, 4)
                spots = [(2 * ax + v) * 4 + ny for v in range(2)]
            else:
                spots = [(2 * ax + v // 2) * 4 + 2 * ay + v % 2 for v in range(4)]
            remainder = remainder + fold(acc[:, L:], spots, 1 + 2 * axis + side)
        if axis == 2:
            rows[at, 2] = remainder.astype(BF)
        else:
            rem_out[at] = remainder

    def finish_centre(q):
        ax, ay = q // 2, lax.rem(q, 2)
        at = meta[E + q]
        acc = gather(x0, q, range(8))
        rows[at, 0] = acc[:, :L].astype(BF)
        raw = acc[:, L:]
        spots = [(2 * ax + v // 2) * 4 + 2 * ay + v % 2 for v in range(4)]
        moved = pltpu.roll(raw, 49 - 112 + L, 1)
        rem_out[at] = jnp.where(lane == 49, moved, fold(raw, spots, 0))

    for at_step, (k, outer) in enumerate(kinds):

        @pl.when(step == at_step)
        def _(k=k, outer=outer):
            def run(q, carry):
                if k == 0:
                    direct(q)
                elif outer:
                    outside(k, q)
                else:
                    same(k, q)
                if outer and k % 2 == 0:
                    finish_sides((k - 1) // 2, q)
                if k == 6 and not outer:
                    finish_centre(q)
                return carry

            lax.fori_loop(0, 4, run, 0)


SCRATCH = [
    pltpu.VMEM((H * PE, L), F32),
    pltpu.VMEM((H * PE, L), F32),
]
HALF = pltpu.VMEM((E, H, 2 * L), BF)
FULL = pltpu.VMEM((E, H, 2 * L), F32)
REST = jax.ShapeDtypeStruct((4, H, L), F32)


def centre_kernel(scal, meta, jac, pz0, pz1, pt, res_t, rows, rem_out, main, rest, x0, keep):
    block_kernel(
        [(k, False) for k in range(7)], scal, meta, jac, (pz0, pz1), {}, pt, res_t, None,
        rows, rem_out, (main, rest, x0, None, keep),
    )


def sides_kernel(
    scal, meta, jac, pz0, pz1, pt, gx, gym, gyp, rem_in, started, rows, rem_out, main, rest, xs
):
    block_kernel(
        [(k, True) for k in range(1, 5)], scal, meta, jac, (pz0, pz1),
        {1: gx, 2: gx, 3: gym, 4: gyp}, pt, None, rem_in,
        rows, rem_out, (main, rest, None, xs, None),
    )


def depth_kernel(scal, meta, jac, pt, gzm, gzp, rem_in, rows, main, rest, xs):
    block_kernel(
        [(k, True) for k in (5, 6)], scal, meta, jac, None,
        {5: gzm, 6: gzp}, pt, None, rem_in,
        rows, None, (main, rest, None, xs, None),
    )


def block_call(kernel, steps, start, operands, out_shape, out_specs, scratch, name, aliases, cost):
    in_specs = [smem(), smem(), pl.BlockSpec((1, W, E, W), lambda s: (start + s, 0, 0, 0))]
    in_specs += [vmem()] * (len(operands) - 3)
    if aliases:
        in_specs[-1] = pl.BlockSpec(memory_space=pl.ANY)
    return pl.pallas_call(
        kernel,
        grid=(steps,),
        in_specs=in_specs,
        out_specs=out_specs,
        out_shape=out_shape,
        scratch_shapes=SCRATCH + scratch,
        input_output_aliases=aliases,
        compiler_params=pltpu.CompilerParams(vmem_limit_bytes=VMEM_LIMIT),
        cost_estimate=pl.CostEstimate(flops=cost, bytes_accessed=1_000_000, transcendentals=0),
        name=name,
    )(*operands)


def final_kernel(scal, *refs):
    parts = [refs[5 * p : 5 * p + 5] for p in range(3)]
    coarse, restricted, s1, s2 = refs[15:]
    step = pl.program_id(0)
    lane = lax.broadcasted_iota(jnp.int32, (H, L), 1)

    def plane_of(part, slot):
        z, y = slot // 4, slot % 4
        which, row = [(0, z), (1, z), (3 + z // 2, z % 2), (2, z)][y]
        return parts[part][which][row, 0].astype(F32)

    @pl.when(scal[4] == 0)
    def _():
        coarse[...] = jnp.zeros_like(coarse)
        restricted[...] = jnp.zeros_like(restricted)

    @pl.when(scal[4] == 1)
    def _():
        @pl.when(step == 0)
        def _():
            acc = jnp.zeros((H, L), F32)
            for slot in range(16):
                turned = pltpu.roll(plane_of(2, slot), (slot - 49 + L) % L, 1)
                acc = jnp.where(lane == slot, turned, acc)
            restricted[...] = acc.T[:16, :W].astype(BF)

        for k in range(7):

            @pl.when(step == k)
            def _(k=k):
                for slot in range(16):
                    s1[pl.ds(slot, H, stride=PS), :] = plane_of(0 if k < 5 else 1, slot)
                    tail = plane_of(2, slot)
                    s2[pl.ds(slot, H, stride=PS), :] = pltpu.roll(tail, L - R * k, 1) if k else tail

        def write(i, carry):
            for u in range(9):
                row = i * 9 + u
                at = pl.ds(row * PS, 16)
                coarse[0, row] = jnp.concatenate([s1[at, :], s2[at, :R]], axis=1).astype(BF)
            return carry

        lax.fori_loop(0, W // 9, write, 0)


def final_call(scal, first, second):
    def plane_spec(array, index):
        return pl.BlockSpec((array.shape[0], 1, H, L), lambda s: (0, index(s), 0, 0))

    specs = [plane_spec(a, lambda s: jnp.where(s == 0, 4, jnp.minimum(s, 4) - 1)) for a in first]
    specs += [plane_spec(a, lambda s: jnp.maximum(s - 5, 0)) for a in second]
    specs += [plane_spec(a, lambda s: 2) for a in second]
    return pl.pallas_call(
        final_kernel,
        grid=(7,),
        in_specs=[smem()] + specs,
        out_specs=[pl.BlockSpec((1, W, 16, W), lambda s: (s, 0, 0, 0)), vmem()],
        out_shape=[jax.ShapeDtypeStruct((7, W, 16, W), BF), jax.ShapeDtypeStruct((16, W), BF)],
        scratch_shapes=[pltpu.VMEM((H * PS, L), F32), pltpu.VMEM((H * PS, L), F32)],
        compiler_params=pltpu.CompilerParams(vmem_limit_bytes=VMEM_LIMIT),
        name="assemble",
    )(scal, *first, *second, *second)


DOWN = [(1, 0), (2, 1), (3, 2), (0, 3)]
UP = [(3, 0), (0, 1), (1, 2), (2, 3)]


def to_owner_row(rows):
    return lax.all_to_all(rows, "zz", split_axis=0, concat_axis=0, tiled=True)


def along_ring(held):
    down = lax.ppermute(held, "yy", DOWN)
    up = lax.ppermute(held, "yy", UP)
    return down, up


def forward(down, up):
    return lax.ppermute(down[:2], "yy", [(1, 0)]), lax.ppermute(up[2:], "yy", [(3, 0)])


def body(jacobian, prolong, residual, neighbours, agg_map, owners):
    gx, gy = lax.axis_index("gx"), lax.axis_index("gy")
    zz, yy = lax.axis_index("zz"), lax.axis_index("yy")
    device = (gx * 4 + gy) * 16 + zz * 4 + yy
    scal = jnp.stack(
        [device * E, device * 4, zz, gx, (yy == 0).astype(jnp.int32), gy, yy]
    ).astype(jnp.int32)
    jac = jnp.transpose(jacobian, (1, 2, 0, 3))
    pro = jnp.transpose(prolong, (1, 0, 2))
    res_t = jnp.pad(residual.T.astype(F32), ((0, 1), (0, L - E)))
    meta, pz0, pz1, xs, ys0, ys1, pt = pack_call(scal, neighbours.T, agg_map, owners, pro)
    gz = ("zz", "yy")
    ghost_x = lax.ppermute(xs, "gx", [(0, 1), (1, 0)])
    ghost_zm = lax.ppermute(pz1, gz, [(i, (i + 1) % 16) for i in range(16)])
    ghost_zp = lax.ppermute(pz0, gz, [((i + 1) % 16, i) for i in range(16)])
    ghost_ym = lax.ppermute(ys1, "gy", [(i, (i + 1) % 4) for i in range(4)])
    ghost_yp = lax.ppermute(ys0, "gy", [((i + 1) % 4, i) for i in range(4)])
    five = jax.ShapeDtypeStruct((4, 5, H, L), BF)
    first, rem = block_call(
        centre_kernel, 7, 0, (scal, meta, jac, pz0, pz1, pt, res_t),
        [five, REST], [pl.BlockSpec((4, 1, H, L), lambda s: (0, 4, 0, 0)), vmem()],
        [HALF, FULL], "centre", {}, 18_000_000_000,
    )
    first, rem = block_call(
        sides_kernel, 4, 1,
        (scal, meta, jac, pz0, pz1, pt, ghost_x, ghost_ym, ghost_yp, rem, first),
        [five, REST], [pl.BlockSpec((4, 4, H, L), lambda s: (0, 0, 0, 0)), vmem()],
        [HALF], "sides", {10: 0}, 12_000_000_000,
    )
    held1 = to_owner_row(first)
    second = block_call(
        depth_kernel, 2, 5, (scal, meta, jac, pt, ghost_zm, ghost_zp, rem),
        jax.ShapeDtypeStruct((4, 3, H, L), BF), vmem(),
        [HALF], "depth", {}, 9_000_000_000,
    )
    held1, second = lax.optimization_barrier((held1, second))
    down1, up1 = along_ring(held1)
    held2 = to_owner_row(second)
    twice1 = forward(down1, up1)
    down2, up2 = along_ring(held2)
    twice2 = forward(down2, up2)
    coarse, restricted = final_call(scal, (held1, down1, up1) + twice1, (held2, down2, up2) + twice2)
    return jnp.transpose(coarse, (2, 0, 1, 3)), restricted


def solution(mesh):
    fine = Mesh(mesh.devices.reshape(2, 4, 4, 4), ("gx", "gy", "zz", "yy"))
    every = ("gx", "gy", "zz", "yy")
    return jax.shard_map(
        body,
        mesh=fine,
        in_specs=(P(every), P(every), P(every), P(every), P(every), P(every)),
        out_specs=(P(every), P(every)),
        check_vma=False,
    )
```

```python
import functools

import jax
import jax.numpy as jnp
from jax import lax
from jax.experimental import pallas as pl
from jax.experimental.pallas import tpu as pltpu
from jax.sharding import Mesh, PartitionSpec as P

E = 32
W = 135
H = 136
L = 128
R = W - L
PE = 36
PS = 20
BF = jnp.bfloat16
F32 = jnp.float32
VMEM_LIMIT = 40 * 1024 * 1024


def anywhere():
    return pl.BlockSpec(memory_space=pl.ANY)


def smem():
    return pl.BlockSpec(memory_space=pltpu.SMEM)


def vmem():
    return pl.BlockSpec(memory_space=pltpu.VMEM)


def spread(block, main, rest):
    def step(i, carry):
        for u in range(5):
            row = i * 5 + u
            values = block(row).astype(F32)
            at = pl.ds(row * PE, E)
            main[at, :] = values[:, :L]
            rest[at, 0:R] = values[:, L:]
        return carry

    lax.fori_loop(0, W // 5, step, 0)


def clear(main, rest):
    main[W * PE : H * PE, :] = jnp.zeros((PE, L), F32)
    rest[...] = jnp.zeros((H * PE, L), F32)


def take(ref, element):
    return ref[pl.ds(element, H, stride=PE), :]


def pack_kernel(scal, nbr, agg, own, p_ref, meta, pz0, pz1, xs, ys0, ys1, pt, main, rest):
    pz, ys = (pz0, pz1), (ys0, ys1)
    base = scal[0]

    def place(e, carry):
        def near(direction):
            local = nbr[direction, e] - base
            here = (local >= 0) & (local < E)
            safe = jnp.clip(local, 0, E - 1)
            same = here & (agg[safe] == agg[e])
            return here.astype(jnp.int32), same.astype(jnp.int32)

        here_xm, odd_x = near(0)
        here_xp, _ = near(1)
        here_ym, odd_y = near(2)
        here_yp, _ = near(3)
        _, odd_z = near(4)
        agg_x = jnp.where(odd_x == 1, 1 - here_xp, here_xm)
        agg_y = jnp.where(odd_y == 1, 1 - here_yp, here_ym)
        meta[odd_z * 16 + (2 * agg_x + odd_x) * 4 + 2 * agg_y + odd_y] = e
        owner = own[agg[e] - scal[1]]
        meta[E + agg_x * 2 + agg_y] = owner // 4
        return carry

    lax.fori_loop(0, E, place, 0)
    clear(main, rest)
    spread(lambda row: p_ref[row], main, rest)
    for oz in range(2):
        plane = jnp.zeros((H, L), F32)
        for xy in range(16):
            e = meta[oz * 16 + xy]
            a = take(main, e)
            b = take(rest, e)
            pz[oz][xy] = a.astype(BF)
            plane = plane + (pltpu.roll(b, R * xy, 1) if xy else b)
            pt[oz * 16 + xy] = jnp.concatenate([a.T, b.T[:8]], axis=0).astype(BF)
        pz[oz][16] = plane.astype(BF)
    face = jnp.where(scal[3] == 0, 12, 0)
    for oz in range(2):
        for v in range(4):
            xs[oz * 4 + v] = pz[oz][face + v]
            ys[0][oz * 4 + v] = pz[oz][v * 4]
            ys[1][oz * 4 + v] = pz[oz][v * 4 + 3]
        xs[8 + oz] = pz[oz][16]
        ys[0][8 + oz] = pz[oz][16]
        ys[1][8 + oz] = pz[oz][16]


def pack_call(*operands):
    return pl.pallas_call(
        pack_kernel,
        in_specs=[smem()] * 4 + [vmem()],
        out_specs=[smem()] + [vmem()] * 6,
        out_shape=[
            jax.ShapeDtypeStruct((40,), jnp.int32),
            jax.ShapeDtypeStruct((17, H, L), BF),
            jax.ShapeDtypeStruct((17, H, L), BF),
            jax.ShapeDtypeStruct((10, H, L), BF),
            jax.ShapeDtypeStruct((10, H, L), BF),
            jax.ShapeDtypeStruct((10, H, L), BF),
            jax.ShapeDtypeStruct((E, H, H), BF),
        ],
        scratch_shapes=[pltpu.VMEM((H * PE, L), F32), pltpu.VMEM((H * PE, L), F32)],
        compiler_params=pltpu.CompilerParams(vmem_limit_bytes=VMEM_LIMIT),
        name="pack",
    )(*operands)


DEPTH = 3


def block_kernel(kinds, scal, meta, jac, early, late, views, rows, rows_out, rem_out, rem_to, buffers):
    jbuf, main, rest, x0, xs, keep, jac_sems, early_sems, late_sems, out_sems = buffers
    pz, ghosts, pt, res_t, rem_in = views
    lane = lax.broadcasted_iota(jnp.int32, (H, L), 1)

    def jac_copy(i):
        return pltpu.make_async_copy(jac.at[kinds[i][0]], jbuf.at[i % DEPTH], jac_sems.at[i % DEPTH])

    early_copies = [pltpu.make_async_copy(a, b, early_sems.at[i]) for i, (a, b) in enumerate(early)]
    late_copies = [pltpu.make_async_copy(a, b, late_sems.at[i]) for i, (a, b) in enumerate(late)]
    jac_copy(0).start()
    for copy in early_copies:
        copy.start()
    jac_copy(1).start()
    for copy in late_copies:
        copy.start()
    if len(kinds) > 2:
        jac_copy(2).start()
    clear(main, rest)

    def product(c, plane_main, plane_rest, idx):
        e = meta[c]
        left = jnp.concatenate([take(main, e), take(rest, e)[:, :8]], axis=1).astype(BF)
        right = jnp.concatenate([plane_main, plane_rest], axis=1)
        out = jnp.dot(left, right, preferred_element_type=F32)
        low = R * idx
        good = (lane >= low) & (lane < low + R)
        return jnp.concatenate([out[:, :L], jnp.where(good, out[:, L:], 0.0)], axis=1)

    def where_is(q, octant):
        ax, ay = q // 2, lax.rem(q, 2)
        ox, oy, oz = octant // 4, octant // 2 % 2, octant % 2
        return 2 * ax + ox, 2 * ay + oy, oz

    def bits(octant):
        return octant // 4, octant // 2 % 2, octant % 2

    def direct(q):
        for octant in range(8):
            x, y, oz = where_is(q, octant)
            idx = x * 4 + y
            keep[q * 8 + octant] = product(oz * 16 + idx, pz[oz][idx], pz[oz][16], idx)

    def same(k, q):
        axis, shift = (k - 1) // 2, -1 if k % 2 else 1
        for octant in range(8):
            if bits(octant)[axis] != (1 if shift < 0 else 0):
                continue
            x, y, oz = where_is(q, octant)
            near = [x, y, oz]
            near[axis] = near[axis] + shift
            idx = near[0] * 4 + near[1]
            out = product(oz * 16 + x * 4 + y, pz[near[2]][idx], pz[near[2]][16], idx)
            out = out + keep[q * 8 + octant]
            if axis < 2:
                keep[q * 8 + octant] = out
            else:
                e = meta[oz * 16 + x * 4 + y]
                column = pltpu.roll(res_t[...], lax.rem(112 - e + L, L), 1)
                out = jnp.concatenate([out[:, :L], jnp.where(lane == 112, column, out[:, L:])], axis=1)
                x0[q * 8 + octant] = out.astype(BF)

    def outside(k, q):
        axis, shift = (k - 1) // 2, -1 if k % 2 else 1
        ghost = ghosts[k]
        for octant in range(8):
            if bits(octant)[axis] != (0 if shift < 0 else 1):
                continue
            x, y, oz = where_is(q, octant)
            c = oz * 16 + x * 4 + y
            if axis == 2:
                idx = x * 4 + y
                out = product(c, ghost[idx], ghost[16], idx)
                edge = 0 if shift < 0 else 15
                absent = scal[2] * 4 + scal[6] == edge
            else:
                along, other = (x, y) if axis == 0 else (y, x)
                spot = along + shift
                off = (spot < 0) | (spot > 3)
                spot = lax.rem(spot + 4, 4)
                idx = spot * 4 + other if axis == 0 else other * 4 + spot
                plane_main = jnp.where(off, ghost[oz * 4 + other], pz[oz][idx])
                plane_rest = jnp.where(off, ghost[8 + oz], pz[oz][16])
                out = product(c, plane_main, plane_rest, idx)
                edge = 0 if shift < 0 else (1, 3)[axis]
                absent = off & (scal[(3, 5)[axis]] == edge)
            xs[q * 8 + octant] = (out * jnp.where(absent, 0.0, 1.0)).astype(BF)

    def gather(ref, q, octants):
        acc = None
        for octant in octants:
            x, y, oz = where_is(q, octant)
            part = jnp.dot(pt[oz * 16 + x * 4 + y], ref[q * 8 + octant], preferred_element_type=F32)
            acc = part if acc is None else acc + part
        return acc

    def fold(raw, spots, slot):
        total = None
        for spot in spots:
            turned = pltpu.roll(raw, lax.rem(R * slot - R * spot + 2 * L, L), 1)
            total = turned if total is None else total + turned
        good = (lane >= R * slot) & (lane < R * slot + R)
        return jnp.where(good, total, 0.0)

    def finish_sides(axis, q):
        ax, ay = q // 2, lax.rem(q, 2)
        at = meta[E + q]
        remainder = (rem_out if axis == 1 else rem_in)[at]
        for side in range(2):
            acc = gather(xs, q, [o for o in range(8) if bits(o)[axis] == side])
            rows[at, 2 * (axis % 2) + side] = acc[:, :L].astype(BF)
            if axis == 0:
                nx = lax.rem(2 * ax + (-1 if side == 0 else 2) + 4, 4)
                spots = [nx * 4 + 2 * ay + v for v in range(2)]
            elif axis == 1:
                ny = lax.rem(2 * ay + (-1 if side == 0 else 2) + 4, 4)
                spots = [(2 * ax + v) * 4 + ny for v in range(2)]
            else:
                spots = [(2 * ax + v // 2) * 4 + 2 * ay + v % 2 for v in range(4)]
            remainder = remainder + fold(acc[:, L:], spots, 1 + 2 * axis + side)
        if axis == 2:
            rows[at, 2] = remainder.astype(BF)
        else:
            rem_out[at] = remainder

    def finish_centre(q):
        ax, ay = q // 2, lax.rem(q, 2)
        at = meta[E + q]
        acc = gather(x0, q, range(8))
        rows[at, 0] = acc[:, :L].astype(BF)
        raw = acc[:, L:]
        spots = [(2 * ax + v // 2) * 4 + 2 * ay + v % 2 for v in range(4)]
        moved = pltpu.roll(raw, 49 - 112 + L, 1)
        rem_out[at] = jnp.where(lane == 49, moved, fold(raw, spots, 0))

    for i, (k, outer) in enumerate(kinds):
        jac_copy(i).wait()
        spread(lambda row, i=i: jbuf[i % DEPTH, row], main, rest)
        if i + DEPTH < len(kinds):
            jac_copy(i + DEPTH).start()
        if i == 0:
            for copy in early_copies:
                copy.wait()
        if i == 1:
            for copy in late_copies:
                copy.wait()

        def run(q, carry, k=k, outer=outer):
            if k == 0:
                direct(q)
            elif outer:
                outside(k, q)
            else:
                same(k, q)
            if outer and k % 2 == 0:
                finish_sides((k - 1) // 2, q)
            if k == 6 and not outer:
                finish_centre(q)
            return carry

        lax.fori_loop(0, 4, run, 0)
    copies = [pltpu.make_async_copy(rows, rows_out, out_sems.at[0])]
    if rem_out is not None:
        copies.append(pltpu.make_async_copy(rem_out, rem_to, out_sems.at[1]))
    for copy in copies:
        copy.start()
    for copy in copies:
        copy.wait()


COMMON = [
    pltpu.VMEM((DEPTH, W, E, W), BF),
    pltpu.VMEM((H * PE, L), F32),
    pltpu.VMEM((H * PE, L), F32),
    pltpu.SemaphoreType.DMA((DEPTH,)),
    pltpu.SemaphoreType.DMA((6,)),
    pltpu.SemaphoreType.DMA((6,)),
    pltpu.SemaphoreType.DMA((2,)),
]
HALF = pltpu.VMEM((E, H, 2 * L), BF)
FULL = pltpu.VMEM((E, H, 2 * L), F32)
REM = pltpu.VMEM((4, H, L), F32)
REST = jax.ShapeDtypeStruct((4, H, L), F32)


def centre_kernel(scal, meta, jac, pz0, pz1, pt, res_t, rows_out, rem_to, *scratch):
    jbuf, main, rest, j_sems, e_sems, l_sems, o_sems, x0, keep, vz0, vz1, vpt, vres, rows, rem_out = scratch
    block_kernel(
        [(k, False) for k in range(7)], scal, meta, jac,
        [(pz0, vz0), (pz1, vz1)], [(pt, vpt), (res_t, vres)],
        ((vz0, vz1), {}, vpt, vres, None),
        rows, rows_out.at[:, pl.ds(4, 1)], rem_out, rem_to,
        (jbuf, main, rest, x0, None, keep, j_sems, e_sems, l_sems, o_sems),
    )


def sides_kernel(scal, meta, jac, pz0, pz1, pt, gx, gym, gyp, rem_in, started, rows_out, rem_to, *scratch):
    jbuf, main, rest, j_sems, e_sems, l_sems, o_sems = scratch[:7]
    xs, vz0, vz1, vpt, vx, vym, vyp, vrem, rows, rem_out = scratch[7:]
    block_kernel(
        [(k, True) for k in range(1, 5)], scal, meta, jac,
        [(pz0, vz0), (pz1, vz1), (gx, vx)], [(pt, vpt), (rem_in, vrem), (gym, vym), (gyp, vyp)],
        ((vz0, vz1), {1: vx, 2: vx, 3: vym, 4: vyp}, vpt, None, vrem),
        rows, rows_out.at[:, pl.ds(0, 4)], rem_out, rem_to,
        (jbuf, main, rest, None, xs, None, j_sems, e_sems, l_sems, o_sems),
    )


def depth_kernel(scal, meta, jac, pt, gzm, gzp, rem_in, rows_out, *scratch):
    jbuf, main, rest, j_sems, e_sems, l_sems, o_sems, xs, vpt, vzm, vzp, vrem, rows = scratch
    block_kernel(
        [(k, True) for k in (5, 6)], scal, meta, jac,
        [(gzm, vzm)], [(pt, vpt), (gzp, vzp), (rem_in, vrem)],
        (None, {5: vzm, 6: vzp}, vpt, None, vrem),
        rows, rows_out, None, None,
        (jbuf, main, rest, None, xs, None, j_sems, e_sems, l_sems, o_sems),
    )


def block_call(kernel, operands, out_shape, scratch, name, aliases, cost):
    return pl.pallas_call(
        kernel,
        in_specs=[smem(), smem()] + [anywhere()] * (len(operands) - 2),
        out_specs=jax.tree.map(lambda _: anywhere(), out_shape),
        out_shape=out_shape,
        scratch_shapes=COMMON + scratch,
        input_output_aliases=aliases,
        compiler_params=pltpu.CompilerParams(vmem_limit_bytes=VMEM_LIMIT),
        cost_estimate=pl.CostEstimate(flops=cost, bytes_accessed=1_000_000, transcendentals=0),
        name=name,
    )(*operands)


def final_kernel(scal, *refs):
    sources = refs[:10]
    coarse, restricted = refs[10:12]
    held = refs[12:22]
    out, s1, s2, in_sems, out_sems = refs[22:]
    lane = lax.broadcasted_iota(jnp.int32, (H, L), 1)

    def copies(n):
        part, plane = (0, n) if n < 5 else (1, n - 5)
        return [
            pltpu.make_async_copy(
                sources[5 * part + i].at[:, plane], held[5 * part + i].at[:, plane], in_sems.at[n, i]
            )
            for i in range(5)
        ]

    def plane_of(n, slot):
        part, plane = (0, n) if n < 5 else (1, n - 5)
        z, y = slot // 4, slot % 4
        which, row = [(0, z), (1, z), (3 + z // 2, z % 2), (2, z)][y]
        return held[5 * part + which][row, plane].astype(F32)

    def out_copy(k):
        return pltpu.make_async_copy(out.at[k % 2], coarse.at[k], out_sems.at[k])

    @pl.when(scal[4] == 0)
    def _():
        out[0] = jnp.zeros((W, 16, W), BF)
        restricted[...] = jnp.zeros_like(restricted)
        zero_copies = [pltpu.make_async_copy(out.at[0], coarse.at[k], out_sems.at[k]) for k in range(7)]
        for copy in zero_copies:
            copy.start()
        for copy in zero_copies:
            copy.wait()

    @pl.when(scal[4] == 1)
    def _():
        order = [4, 0, 1, 2, 3, 5, 6]
        for n in [7] + order:
            for copy in copies(n):
                copy.start()
        for copy in copies(7):
            copy.wait()
        acc = jnp.zeros((H, L), F32)
        for slot in range(16):
            turned = pltpu.roll(plane_of(7, slot), (slot - 49 + L) % L, 1)
            acc = jnp.where(lane == slot, turned, acc)
        restricted[...] = acc.T[:16, :W].astype(BF)
        for k in range(7):
            for copy in copies(order[k]):
                copy.wait()
            for slot in range(16):
                s1[pl.ds(slot, H, stride=PS), :] = plane_of(order[k], slot)
                tail = plane_of(7, slot)
                s2[pl.ds(slot, H, stride=PS), :] = pltpu.roll(tail, L - R * k, 1) if k else tail
            if k >= 2:
                out_copy(k - 2).wait()

            def write(i, carry, k=k):
                for u in range(9):
                    row = i * 9 + u
                    at = pl.ds(row * PS, 16)
                    out[k % 2, row] = jnp.concatenate([s1[at, :], s2[at, :R]], axis=1).astype(BF)
                return carry

            lax.fori_loop(0, W // 9, write, 0)
            out_copy(k).start()
        out_copy(5).wait()
        out_copy(6).wait()


def final_call(scal, first, second):
    operands = [scal, *first, *second]
    return pl.pallas_call(
        final_kernel,
        in_specs=[smem()] + [anywhere()] * 10,
        out_specs=[anywhere(), vmem()],
        out_shape=[jax.ShapeDtypeStruct((7, W, 16, W), BF), jax.ShapeDtypeStruct((16, W), BF)],
        scratch_shapes=[pltpu.VMEM(a.shape, BF) for a in operands[1:]]
        + [
            pltpu.VMEM((2, W, 16, W), BF),
            pltpu.VMEM((H * PS, L), F32),
            pltpu.VMEM((H * PS, L), F32),
            pltpu.SemaphoreType.DMA((8, 5)),
            pltpu.SemaphoreType.DMA((7,)),
        ],
        compiler_params=pltpu.CompilerParams(vmem_limit_bytes=VMEM_LIMIT),
        name="assemble",
    )(*operands)


DOWN = [(1, 0), (2, 1), (3, 2), (0, 3)]
UP = [(3, 0), (0, 1), (1, 2), (2, 3)]


def to_owner_row(rows):
    return lax.all_to_all(rows, "zz", split_axis=0, concat_axis=0, tiled=True)


def along_ring(held):
    down = lax.ppermute(held, "yy", DOWN)
    up = lax.ppermute(held, "yy", UP)
    return down, up


def forward(down, up):
    return lax.ppermute(down[:2], "yy", [(1, 0)]), lax.ppermute(up[2:], "yy", [(3, 0)])


def body(jacobian, prolong, residual, neighbours, agg_map, owners):
    gx, gy = lax.axis_index("gx"), lax.axis_index("gy")
    zz, yy = lax.axis_index("zz"), lax.axis_index("yy")
    device = (gx * 4 + gy) * 16 + zz * 4 + yy
    scal = jnp.stack(
        [device * E, device * 4, zz, gx, (yy == 0).astype(jnp.int32), gy, yy]
    ).astype(jnp.int32)
    jac = jnp.transpose(jacobian, (1, 2, 0, 3))
    pro = jnp.transpose(prolong, (1, 0, 2))
    res_t = jnp.pad(residual.T.astype(F32), ((0, 1), (0, L - E)))
    meta, pz0, pz1, xs, ys0, ys1, pt = pack_call(scal, neighbours.T, agg_map, owners, pro)
    gz = ("zz", "yy")
    ghost_x = lax.ppermute(xs, "gx", [(0, 1), (1, 0)])
    ghost_zm = lax.ppermute(pz1, gz, [(i, (i + 1) % 16) for i in range(16)])
    ghost_zp = lax.ppermute(pz0, gz, [((i + 1) % 16, i) for i in range(16)])
    ghost_ym = lax.ppermute(ys1, "gy", [(i, (i + 1) % 4) for i in range(4)])
    ghost_yp = lax.ppermute(ys0, "gy", [((i + 1) % 4, i) for i in range(4)])
    five = jax.ShapeDtypeStruct((4, 5, H, L), BF)
    z_face, side_face = [pltpu.VMEM((n, H, L), BF) for n in (17, 10)]
    turned = pltpu.VMEM((E, H, H), BF)
    first, rem = block_call(
        centre_kernel, (scal, meta, jac, pz0, pz1, pt, res_t), [five, REST],
        [HALF, FULL, z_face, z_face, turned, pltpu.VMEM((H, L), F32), pltpu.VMEM((4, 1, H, L), BF), REM],
        "centre", {}, 18_000_000_000,
    )
    first, rem = block_call(
        sides_kernel, (scal, meta, jac, pz0, pz1, pt, ghost_x, ghost_ym, ghost_yp, rem, first), [five, REST],
        [HALF, z_face, z_face, turned, side_face, side_face, side_face, REM, pltpu.VMEM((4, 4, H, L), BF), REM],
        "sides", {10: 0}, 12_000_000_000,
    )
    held1 = to_owner_row(first)
    (second,) = block_call(
        depth_kernel, (scal, meta, jac, pt, ghost_zm, ghost_zp, rem),
        [jax.ShapeDtypeStruct((4, 3, H, L), BF)],
        [HALF, turned, z_face, z_face, REM, pltpu.VMEM((4, 3, H, L), BF)],
        "depth", {}, 9_000_000_000,
    )
    held1, second = lax.optimization_barrier((held1, second))
    down1, up1 = along_ring(held1)
    held2 = to_owner_row(second)
    twice1 = forward(down1, up1)
    down2, up2 = along_ring(held2)
    twice2 = forward(down2, up2)
    coarse, restricted = final_call(scal, (held1, down1, up1) + twice1, (held2, down2, up2) + twice2)
    return jnp.transpose(coarse, (2, 0, 1, 3)), restricted


def solution(mesh):
    fine = Mesh(mesh.devices.reshape(2, 4, 4, 4), ("gx", "gy", "zz", "yy"))
    every = ("gx", "gy", "zz", "yy")
    return jax.shard_map(
        body,
        mesh=fine,
        in_specs=(P(every), P(every), P(every), P(every), P(every), P(every)),
        out_specs=(P(every), P(every)),
        check_vma=False,
    )
```

```python
import functools

import jax
import jax.numpy as jnp
from jax import lax
from jax.experimental import pallas as pl
from jax.experimental.pallas import tpu as pltpu
from jax.sharding import Mesh, PartitionSpec as P

E = 32
W = 135
H = 136
L = 128
R = W - L
PE = 36
PS = 20
BF = jnp.bfloat16
F32 = jnp.float32
VMEM_LIMIT = 40 * 1024 * 1024
PACK_LIMIT = 40 * 1024 * 1024


def anywhere():
    return pl.BlockSpec(memory_space=pl.ANY)


def smem():
    return pl.BlockSpec(memory_space=pltpu.SMEM)


def vmem():
    return pl.BlockSpec(memory_space=pltpu.VMEM)


def spread(block, main, rest):
    def step(i, carry):
        for u in range(5):
            row = i * 5 + u
            values = block(row).astype(F32)
            at = pl.ds(row * PE, E)
            main[at, :] = values[:, :L]
            rest[at, 0:R] = values[:, L:]
        return carry

    lax.fori_loop(0, W // 5, step, 0)


def clear(main, rest):
    main[W * PE : H * PE, :] = jnp.zeros((PE, L), F32)
    rest[...] = jnp.zeros((H * PE, L), F32)


def take(ref, element):
    return ref[pl.ds(element, H, stride=PE), :]


def pack_kernel(scal, nbr, agg, own, p_ref, meta, pz0, pz1, xs, ys0, ys1, pt, main, rest):
    pz, ys = (pz0, pz1), (ys0, ys1)
    base = scal[0]

    def place(e, carry):
        def near(direction):
            local = nbr[direction, e] - base
            here = (local >= 0) & (local < E)
            safe = jnp.clip(local, 0, E - 1)
            same = here & (agg[safe] == agg[e])
            return here.astype(jnp.int32), same.astype(jnp.int32)

        here_xm, odd_x = near(0)
        here_xp, _ = near(1)
        here_ym, odd_y = near(2)
        here_yp, _ = near(3)
        _, odd_z = near(4)
        agg_x = jnp.where(odd_x == 1, 1 - here_xp, here_xm)
        agg_y = jnp.where(odd_y == 1, 1 - here_yp, here_ym)
        meta[odd_z * 16 + (2 * agg_x + odd_x) * 4 + 2 * agg_y + odd_y] = e
        owner = own[agg[e] - scal[1]]
        meta[E + agg_x * 2 + agg_y] = owner // 4
        return carry

    lax.fori_loop(0, E, place, 0)
    clear(main, rest)
    spread(lambda row: p_ref[row], main, rest)
    for oz in range(2):
        plane = jnp.zeros((H, L), F32)
        for xy in range(16):
            e = meta[oz * 16 + xy]
            a = take(main, e)
            b = take(rest, e)
            pz[oz][xy] = a.astype(BF)
            plane = plane + (pltpu.roll(b, R * xy, 1) if xy else b)
            pt[oz * 16 + xy] = jnp.concatenate([a.T, b.T[:8]], axis=0).astype(BF)
        pz[oz][16] = plane.astype(BF)
    face = jnp.where(scal[3] == 0, 12, 0)
    for oz in range(2):
        for v in range(4):
            xs[oz * 4 + v] = pz[oz][face + v]
            ys[0][oz * 4 + v] = pz[oz][v * 4]
            ys[1][oz * 4 + v] = pz[oz][v * 4 + 3]
        xs[8 + oz] = pz[oz][16]
        ys[0][8 + oz] = pz[oz][16]
        ys[1][8 + oz] = pz[oz][16]


def pack_call(*operands):
    return pl.pallas_call(
        pack_kernel,
        in_specs=[smem()] * 4 + [vmem()],
        out_specs=[smem()] + [vmem()] * 6,
        out_shape=[
            jax.ShapeDtypeStruct((40,), jnp.int32),
            jax.ShapeDtypeStruct((17, H, L), BF),
            jax.ShapeDtypeStruct((17, H, L), BF),
            jax.ShapeDtypeStruct((10, H, L), BF),
            jax.ShapeDtypeStruct((10, H, L), BF),
            jax.ShapeDtypeStruct((10, H, L), BF),
            jax.ShapeDtypeStruct((E, H, H), BF),
        ],
        scratch_shapes=[pltpu.VMEM((H * PE, L), F32), pltpu.VMEM((H * PE, L), F32)],
        compiler_params=pltpu.CompilerParams(vmem_limit_bytes=PACK_LIMIT),
        name="pack",
    )(*operands)


DEPTH = 3


def block_kernel(kinds, scal, meta, jac, early, late, views, rows, rows_out, rem_out, rem_to, buffers):
    jbuf, main, rest, x0, xs, keep, jac_sems, early_sems, late_sems, out_sems = buffers
    pz, ghosts, pt, (res, res_t), rem_in = views
    lane = lax.broadcasted_iota(jnp.int32, (H, L), 1)

    def jac_copy(i):
        return pltpu.make_async_copy(jac.at[kinds[i][0]], jbuf.at[i % DEPTH], jac_sems.at[i % DEPTH])

    early_copies = [pltpu.make_async_copy(a, b, early_sems.at[i]) for i, (a, b) in enumerate(early)]
    late_copies = [pltpu.make_async_copy(a, b, late_sems.at[i]) for i, (a, b) in enumerate(late)]
    jac_copy(0).start()
    for copy in early_copies:
        copy.start()
    jac_copy(1).start()
    for copy in late_copies:
        copy.start()
    if len(kinds) > 2:
        jac_copy(2).start()
    clear(main, rest)

    def product(c, plane_main, plane_rest, idx):
        e = meta[c]
        left = jnp.concatenate([take(main, e), take(rest, e)[:, :8]], axis=1).astype(BF)
        right = jnp.concatenate([plane_main, plane_rest], axis=1)
        out = jnp.dot(left, right, preferred_element_type=F32)
        low = R * idx
        good = (lane >= low) & (lane < low + R)
        return jnp.concatenate([out[:, :L], jnp.where(good, out[:, L:], 0.0)], axis=1)

    def where_is(q, octant):
        ax, ay = q // 2, lax.rem(q, 2)
        ox, oy, oz = octant // 4, octant // 2 % 2, octant % 2
        return 2 * ax + ox, 2 * ay + oy, oz

    def bits(octant):
        return octant // 4, octant // 2 % 2, octant % 2

    def direct(q):
        for octant in range(8):
            x, y, oz = where_is(q, octant)
            idx = x * 4 + y
            keep[q * 8 + octant] = product(oz * 16 + idx, pz[oz][idx], pz[oz][16], idx)

    def same(k, q):
        axis, shift = (k - 1) // 2, -1 if k % 2 else 1
        for octant in range(8):
            if bits(octant)[axis] != (1 if shift < 0 else 0):
                continue
            x, y, oz = where_is(q, octant)
            near = [x, y, oz]
            near[axis] = near[axis] + shift
            idx = near[0] * 4 + near[1]
            out = product(oz * 16 + x * 4 + y, pz[near[2]][idx], pz[near[2]][16], idx)
            out = out + keep[q * 8 + octant]
            if axis < 2:
                keep[q * 8 + octant] = out
            else:
                e = meta[oz * 16 + x * 4 + y]
                column = pltpu.roll(res_t[...], lax.rem(112 - e + L, L), 1)
                out = jnp.concatenate([out[:, :L], jnp.where(lane == 112, column, out[:, L:])], axis=1)
                x0[q * 8 + octant] = out.astype(BF)

    def outside(k, q):
        axis, shift = (k - 1) // 2, -1 if k % 2 else 1
        ghost = ghosts[k]
        for octant in range(8):
            if bits(octant)[axis] != (0 if shift < 0 else 1):
                continue
            x, y, oz = where_is(q, octant)
            c = oz * 16 + x * 4 + y
            if axis == 2:
                idx = x * 4 + y
                out = product(c, ghost[idx], ghost[16], idx)
                edge = 0 if shift < 0 else 15
                absent = scal[2] * 4 + scal[6] == edge
            else:
                along, other = (x, y) if axis == 0 else (y, x)
                spot = along + shift
                off = (spot < 0) | (spot > 3)
                spot = lax.rem(spot + 4, 4)
                idx = spot * 4 + other if axis == 0 else other * 4 + spot
                plane_main = jnp.where(off, ghost[oz * 4 + other], pz[oz][idx])
                plane_rest = jnp.where(off, ghost[8 + oz], pz[oz][16])
                out = product(c, plane_main, plane_rest, idx)
                edge = 0 if shift < 0 else (1, 3)[axis]
                absent = off & (scal[(3, 5)[axis]] == edge)
            xs[q * 8 + octant] = (out * jnp.where(absent, 0.0, 1.0)).astype(BF)

    def gather(ref, q, octants):
        acc = None
        for octant in octants:
            x, y, oz = where_is(q, octant)
            part = jnp.dot(pt[oz * 16 + x * 4 + y], ref[q * 8 + octant], preferred_element_type=F32)
            acc = part if acc is None else acc + part
        return acc

    def fold(raw, spots, slot):
        total = None
        for spot in spots:
            turned = pltpu.roll(raw, lax.rem(R * slot - R * spot + 2 * L, L), 1)
            total = turned if total is None else total + turned
        good = (lane >= R * slot) & (lane < R * slot + R)
        return jnp.where(good, total, 0.0)

    def finish_sides(axis, q):
        ax, ay = q // 2, lax.rem(q, 2)
        at = meta[E + q]
        remainder = (rem_out if axis == 1 else rem_in)[at]
        for side in range(2):
            acc = gather(xs, q, [o for o in range(8) if bits(o)[axis] == side])
            rows[at, 2 * (axis % 2) + side] = acc[:, :L].astype(BF)
            if axis == 0:
                nx = lax.rem(2 * ax + (-1 if side == 0 else 2) + 4, 4)
                spots = [nx * 4 + 2 * ay + v for v in range(2)]
            elif axis == 1:
                ny = lax.rem(2 * ay + (-1 if side == 0 else 2) + 4, 4)
                spots = [(2 * ax + v) * 4 + ny for v in range(2)]
            else:
                spots = [(2 * ax + v // 2) * 4 + 2 * ay + v % 2 for v in range(4)]
            remainder = remainder + fold(acc[:, L:], spots, 1 + 2 * axis + side)
        if axis == 2:
            rows[at, 2] = remainder.astype(BF)
        else:
            rem_out[at] = remainder

    def finish_centre(q):
        ax, ay = q // 2, lax.rem(q, 2)
        at = meta[E + q]
        acc = gather(x0, q, range(8))
        rows[at, 0] = acc[:, :L].astype(BF)
        raw = acc[:, L:]
        spots = [(2 * ax + v // 2) * 4 + 2 * ay + v % 2 for v in range(4)]
        moved = pltpu.roll(raw, 49 - 112 + L, 1)
        rem_out[at] = jnp.where(lane == 49, moved, fold(raw, spots, 0))

    for i, (k, outer) in enumerate(kinds):
        jac_copy(i).wait()
        spread(lambda row, i=i: jbuf[i % DEPTH, row], main, rest)
        if i + DEPTH < len(kinds):
            jac_copy(i + DEPTH).start()
        if i == 0:
            for copy in early_copies:
                copy.wait()
        if i == 1:
            for copy in late_copies:
                copy.wait()
            if res is not None:
                values = res[...].astype(F32)
                tail = jnp.concatenate([values[:, L:], jnp.zeros((E, L - R), F32)], axis=1)
                res_t[0:L, 0:E] = values[:, :L].T
                res_t[L:H, 0:E] = tail.T[: H - L]

        def run(q, carry, k=k, outer=outer):
            if k == 0:
                direct(q)
            elif outer:
                outside(k, q)
            else:
                same(k, q)
            if outer and k % 2 == 0:
                finish_sides((k - 1) // 2, q)
            if k == 6 and not outer:
                finish_centre(q)
            return carry

        lax.fori_loop(0, 4, run, 0)
    copies = [pltpu.make_async_copy(rows, rows_out, out_sems.at[0])]
    if rem_out is not None:
        copies.append(pltpu.make_async_copy(rem_out, rem_to, out_sems.at[1]))
    for copy in copies:
        copy.start()
    for copy in copies:
        copy.wait()


COMMON = [
    pltpu.VMEM((DEPTH, W, E, W), BF),
    pltpu.VMEM((H * PE, L), F32),
    pltpu.VMEM((H * PE, L), F32),
    pltpu.SemaphoreType.DMA((DEPTH,)),
    pltpu.SemaphoreType.DMA((6,)),
    pltpu.SemaphoreType.DMA((6,)),
    pltpu.SemaphoreType.DMA((2,)),
]
HALF = pltpu.VMEM((E, H, 2 * L), BF)
FULL = pltpu.VMEM((E, H, 2 * L), F32)
REM = pltpu.VMEM((4, H, L), F32)
REST = jax.ShapeDtypeStruct((4, H, L), F32)


def centre_kernel(scal, meta, jac, pz0, pz1, pt, res, rows_out, rem_to, *scratch):
    jbuf, main, rest, j_sems, e_sems, l_sems, o_sems, x0, keep, vz0, vz1, vpt, vres, res_t, rows, rem_out = scratch
    block_kernel(
        [(k, False) for k in range(7)], scal, meta, jac,
        [(pz0, vz0), (pz1, vz1)], [(pt, vpt), (res, vres)],
        ((vz0, vz1), {}, vpt, (vres, res_t), None),
        rows, rows_out.at[:, pl.ds(4, 1)], rem_out, rem_to,
        (jbuf, main, rest, x0, None, keep, j_sems, e_sems, l_sems, o_sems),
    )


def sides_kernel(scal, meta, jac, pz0, pz1, pt, gx, gym, gyp, rem_in, started, rows_out, rem_to, *scratch):
    jbuf, main, rest, j_sems, e_sems, l_sems, o_sems = scratch[:7]
    xs, vz0, vz1, vpt, vx, vym, vyp, vrem, rows, rem_out = scratch[7:]
    block_kernel(
        [(k, True) for k in range(1, 5)], scal, meta, jac,
        [(pz0, vz0), (pz1, vz1), (gx, vx)], [(pt, vpt), (rem_in, vrem), (gym, vym), (gyp, vyp)],
        ((vz0, vz1), {1: vx, 2: vx, 3: vym, 4: vyp}, vpt, (None, None), vrem),
        rows, rows_out.at[:, pl.ds(0, 4)], rem_out, rem_to,
        (jbuf, main, rest, None, xs, None, j_sems, e_sems, l_sems, o_sems),
    )


def depth_kernel(scal, meta, jac, pt, gzm, gzp, rem_in, rows_out, *scratch):
    jbuf, main, rest, j_sems, e_sems, l_sems, o_sems, xs, vpt, vzm, vzp, vrem, rows = scratch
    block_kernel(
        [(k, True) for k in (5, 6)], scal, meta, jac,
        [(gzm, vzm)], [(pt, vpt), (gzp, vzp), (rem_in, vrem)],
        (None, {5: vzm, 6: vzp}, vpt, (None, None), vrem),
        rows, rows_out, None, None,
        (jbuf, main, rest, None, xs, None, j_sems, e_sems, l_sems, o_sems),
    )


def block_call(kernel, operands, out_shape, scratch, name, aliases, cost):
    return pl.pallas_call(
        kernel,
        in_specs=[smem(), smem()] + [anywhere()] * (len(operands) - 2),
        out_specs=jax.tree.map(lambda _: anywhere(), out_shape),
        out_shape=out_shape,
        scratch_shapes=COMMON + scratch,
        input_output_aliases=aliases,
        compiler_params=pltpu.CompilerParams(vmem_limit_bytes=VMEM_LIMIT),
        cost_estimate=pl.CostEstimate(flops=cost, bytes_accessed=1_000_000, transcendentals=0),
        name=name,
    )(*operands)


def final_kernel(scal, *refs):
    held = refs[:10]
    coarse, restricted, out, s1, s2, out_sems = refs[10:]
    lane = lax.broadcasted_iota(jnp.int32, (H, L), 1)

    def plane_of(n, slot):
        part, plane = (0, n) if n < 5 else (1, n - 5)
        z, y = slot // 4, slot % 4
        which, row = [(0, z), (1, z), (3 + z // 2, z % 2), (2, z)][y]
        return held[5 * part + which][row, plane].astype(F32)

    def out_copy(k):
        return pltpu.make_async_copy(out.at[k % 2], coarse.at[k], out_sems.at[k])

    @pl.when(scal[4] == 0)
    def _():
        out[0] = jnp.zeros((W, 16, W), BF)
        restricted[...] = jnp.zeros_like(restricted)
        zero_copies = [pltpu.make_async_copy(out.at[0], coarse.at[k], out_sems.at[k]) for k in range(7)]
        for copy in zero_copies:
            copy.start()
        for copy in zero_copies:
            copy.wait()

    @pl.when(scal[4] == 1)
    def _():
        for k in range(7):
            for slot in range(16):
                s1[pl.ds(slot, H, stride=PS), :] = plane_of([4, 0, 1, 2, 3, 5, 6][k], slot)
                tail = plane_of(7, slot)
                s2[pl.ds(slot, H, stride=PS), :] = pltpu.roll(tail, L - R * k, 1) if k else tail
            if k >= 2:
                out_copy(k - 2).wait()

            def write(i, carry, k=k):
                for u in range(27):
                    row = i * 27 + u
                    at = pl.ds(row * PS, 16)
                    out[k % 2, row] = jnp.concatenate([s1[at, :], s2[at, :R]], axis=1).astype(BF)
                return carry

            lax.fori_loop(0, W // 27, write, 0)
            out_copy(k).start()
        acc = jnp.zeros((H, L), F32)
        for slot in range(16):
            turned = pltpu.roll(plane_of(7, slot), (slot - 49 + L) % L, 1)
            acc = jnp.where(lane == slot, turned, acc)
        restricted[...] = acc.T[:16, :W].astype(BF)
        out_copy(5).wait()
        out_copy(6).wait()


def final_call(scal, rows):
    rows = [pltpu.with_memory_space_constraint(a, pltpu.VMEM) for a in rows]
    return pl.pallas_call(
        final_kernel,
        in_specs=[smem()] + [vmem()] * 10,
        out_specs=[anywhere(), vmem()],
        out_shape=[jax.ShapeDtypeStruct((7, W, 16, W), BF), jax.ShapeDtypeStruct((16, W), BF)],
        scratch_shapes=[
            pltpu.VMEM((2, W, 16, W), BF),
            pltpu.VMEM((H * PS, L), F32),
            pltpu.VMEM((H * PS, L), F32),
            pltpu.SemaphoreType.DMA((7,)),
        ],
        compiler_params=pltpu.CompilerParams(vmem_limit_bytes=VMEM_LIMIT),
        name="assemble",
    )(scal, *rows)


DOWN = [(1, 0), (2, 1), (3, 2), (0, 3)]
UP = [(3, 0), (0, 1), (1, 2), (2, 3)]


def to_owner_row(rows):
    return lax.all_to_all(rows, "zz", split_axis=0, concat_axis=0, tiled=True)


def along_ring(held):
    down = lax.ppermute(held, "yy", DOWN)
    up = lax.ppermute(held, "yy", UP)
    return down, up


def forward(down, up):
    return lax.ppermute(down[:2], "yy", [(1, 0)]), lax.ppermute(up[2:], "yy", [(3, 0)])


def body(jacobian, prolong, residual, neighbours, agg_map, owners):
    gx, gy = lax.axis_index("gx"), lax.axis_index("gy")
    zz, yy = lax.axis_index("zz"), lax.axis_index("yy")
    device = (gx * 4 + gy) * 16 + zz * 4 + yy
    scal = jnp.stack(
        [device * E, device * 4, zz, gx, (yy == 0).astype(jnp.int32), gy, yy]
    ).astype(jnp.int32)
    jac = jnp.transpose(jacobian, (1, 2, 0, 3))
    pro = jnp.transpose(prolong, (1, 0, 2))
    meta, pz0, pz1, xs, ys0, ys1, pt = pack_call(scal, neighbours.T, agg_map, owners, pro)
    gz = ("zz", "yy")
    ghost_x = lax.ppermute(xs, "gx", [(0, 1), (1, 0)])
    ghost_zm = lax.ppermute(pz1, gz, [(i, (i + 1) % 16) for i in range(16)])
    ghost_zp = lax.ppermute(pz0, gz, [((i + 1) % 16, i) for i in range(16)])
    ghost_ym = lax.ppermute(ys1, "gy", [(i, (i + 1) % 4) for i in range(4)])
    ghost_yp = lax.ppermute(ys0, "gy", [((i + 1) % 4, i) for i in range(4)])
    five = jax.ShapeDtypeStruct((4, 5, H, L), BF)
    z_face, side_face = [pltpu.VMEM((n, H, L), BF) for n in (17, 10)]
    turned = pltpu.VMEM((E, H, H), BF)
    first, rem = block_call(
        centre_kernel, (scal, meta, jac, pz0, pz1, pt, residual), [five, REST],
        [HALF, FULL, z_face, z_face, turned, pltpu.VMEM((E, W), BF), pltpu.VMEM((H, L), F32), pltpu.VMEM((4, 1, H, L), BF), REM],
        "centre", {}, 18_000_000_000,
    )
    first, rem = block_call(
        sides_kernel, (scal, meta, jac, pz0, pz1, pt, ghost_x, ghost_ym, ghost_yp, rem, first), [five, REST],
        [HALF, z_face, z_face, turned, side_face, side_face, side_face, REM, pltpu.VMEM((4, 4, H, L), BF), REM],
        "sides", {10: 0}, 12_000_000_000,
    )
    held1 = to_owner_row(first)
    (second,) = block_call(
        depth_kernel, (scal, meta, jac, pt, ghost_zm, ghost_zp, rem),
        [jax.ShapeDtypeStruct((4, 3, H, L), BF)],
        [HALF, turned, z_face, z_face, REM, pltpu.VMEM((4, 3, H, L), BF)],
        "depth", {}, 9_000_000_000,
    )
    held1, second = lax.optimization_barrier((held1, second))
    down1, up1 = along_ring(held1)
    held2 = to_owner_row(second)
    twice1 = forward(down1, up1)
    down2, up2 = along_ring(held2)
    twice2 = forward(down2, up2)
    coarse, restricted = final_call(scal, (held1, down1, up1) + twice1 + (held2, down2, up2) + twice2)
    return jnp.transpose(coarse, (2, 0, 1, 3)), restricted


def solution(mesh):
    fine = Mesh(mesh.devices.reshape(2, 4, 4, 4), ("gx", "gy", "zz", "yy"))
    every = ("gx", "gy", "zz", "yy")
    return jax.shard_map(
        body,
        mesh=fine,
        in_specs=(P(every), P(every), P(every), P(every), P(every), P(every)),
        out_specs=(P(every), P(every)),
        check_vma=False,
    )
```

```python
import functools

import jax
import jax.numpy as jnp
from jax import lax
from jax.experimental import pallas as pl
from jax.experimental.pallas import tpu as pltpu
from jax.sharding import Mesh, PartitionSpec as P

E = 32
W = 135
H = 136
L = 128
R = W - L
PE = 36
PS = 20
BF = jnp.bfloat16
F32 = jnp.float32
VMEM_LIMIT = 40 * 1024 * 1024
PACK_LIMIT = 40 * 1024 * 1024


def anywhere():
    return pl.BlockSpec(memory_space=pl.ANY)


def stay(array):
    return pltpu.with_memory_space_constraint(array, pltpu.HBM)


def smem():
    return pl.BlockSpec(memory_space=pltpu.SMEM)


def vmem():
    return pl.BlockSpec(memory_space=pltpu.VMEM)


def spread(block, main, rest):
    def step(i, carry):
        for u in range(5):
            row = i * 5 + u
            values = block(row).astype(F32)
            at = pl.ds(row * PE, E)
            main[at, :] = values[:, :L]
            rest[at, 0:R] = values[:, L:]
        return carry

    lax.fori_loop(0, W // 5, step, 0)


def clear(main, rest):
    main[W * PE : H * PE, :] = jnp.zeros((PE, L), F32)
    rest[...] = jnp.zeros((H * PE, L), F32)


def take(ref, element):
    return ref[pl.ds(element, H, stride=PE), :]


def pack_kernel(
    scal, nbr_in, agg_in, own_in, p_ref, meta, pz0, pz1, xs, ys0, ys1, pt, main, rest, nbr, agg, own, sems
):
    pz, ys = (pz0, pz1), (ys0, ys1)
    base = scal[0]
    copies = [
        pltpu.make_async_copy(a, b, sems.at[i])
        for i, (a, b) in enumerate([(nbr_in, nbr), (agg_in, agg), (own_in, own)])
    ]
    for copy in copies:
        copy.start()
    clear(main, rest)
    spread(lambda row: p_ref[row], main, rest)
    for copy in copies:
        copy.wait()

    def place(e, carry):
        def near(direction):
            local = nbr[direction, e] - base
            here = (local >= 0) & (local < E)
            safe = jnp.clip(local, 0, E - 1)
            same = here & (agg[safe] == agg[e])
            return here.astype(jnp.int32), same.astype(jnp.int32)

        here_xm, odd_x = near(0)
        here_xp, _ = near(1)
        here_ym, odd_y = near(2)
        here_yp, _ = near(3)
        _, odd_z = near(4)
        agg_x = jnp.where(odd_x == 1, 1 - here_xp, here_xm)
        agg_y = jnp.where(odd_y == 1, 1 - here_yp, here_ym)
        meta[odd_z * 16 + (2 * agg_x + odd_x) * 4 + 2 * agg_y + odd_y] = e
        owner = own[agg[e] - scal[1]]
        meta[E + agg_x * 2 + agg_y] = owner // 4
        return carry

    lax.fori_loop(0, E, place, 0)
    for oz in range(2):
        plane = jnp.zeros((H, L), F32)
        for xy in range(16):
            e = meta[oz * 16 + xy]
            a = take(main, e)
            b = take(rest, e)
            pz[oz][xy] = a.astype(BF)
            plane = plane + (pltpu.roll(b, R * xy, 1) if xy else b)
            pt[oz * 16 + xy] = jnp.concatenate([a.T, b.T[:8]], axis=0).astype(BF)
        pz[oz][16] = plane.astype(BF)
    face = jnp.where(scal[3] == 0, 12, 0)
    for oz in range(2):
        for v in range(4):
            xs[oz * 4 + v] = pz[oz][face + v]
            ys[0][oz * 4 + v] = pz[oz][v * 4]
            ys[1][oz * 4 + v] = pz[oz][v * 4 + 3]
        xs[8 + oz] = pz[oz][16]
        ys[0][8 + oz] = pz[oz][16]
        ys[1][8 + oz] = pz[oz][16]


def pack_call(*operands):
    return pl.pallas_call(
        pack_kernel,
        in_specs=[smem()] + [anywhere()] * 3 + [vmem()],
        out_specs=[smem()] + [vmem()] * 6,
        out_shape=[
            jax.ShapeDtypeStruct((40,), jnp.int32),
            jax.ShapeDtypeStruct((17, H, L), BF),
            jax.ShapeDtypeStruct((17, H, L), BF),
            jax.ShapeDtypeStruct((10, H, L), BF),
            jax.ShapeDtypeStruct((10, H, L), BF),
            jax.ShapeDtypeStruct((10, H, L), BF),
            jax.ShapeDtypeStruct((E, H, H), BF),
        ],
        scratch_shapes=[
            pltpu.VMEM((H * PE, L), F32),
            pltpu.VMEM((H * PE, L), F32),
            pltpu.SMEM((6, E), jnp.int32),
            pltpu.SMEM((E,), jnp.int32),
            pltpu.SMEM((4,), jnp.int32),
            pltpu.SemaphoreType.DMA((3,)),
        ],
        compiler_params=pltpu.CompilerParams(vmem_limit_bytes=PACK_LIMIT),
        name="pack",
    )(*operands)


DEPTH = 3


def block_kernel(kinds, scal, meta, jac, early, late, views, rows, rows_out, rem_out, rem_to, buffers):
    jbuf, main, rest, x0, xs, keep, jac_sems, early_sems, late_sems, out_sems = buffers
    pz, ghosts, pt, (res, res_t), rem_in = views
    lane = lax.broadcasted_iota(jnp.int32, (H, L), 1)

    def jac_copy(i):
        return pltpu.make_async_copy(jac.at[kinds[i][0]], jbuf.at[i % DEPTH], jac_sems.at[i % DEPTH])

    early_copies = [pltpu.make_async_copy(a, b, early_sems.at[i]) for i, (a, b) in enumerate(early)]
    late_copies = [pltpu.make_async_copy(a, b, late_sems.at[i]) for i, (a, b) in enumerate(late)]
    jac_copy(0).start()
    for copy in early_copies:
        copy.start()
    jac_copy(1).start()
    for copy in late_copies:
        copy.start()
    if len(kinds) > 2:
        jac_copy(2).start()
    clear(main, rest)

    def product(c, plane_main, plane_rest, idx):
        e = meta[c]
        left = jnp.concatenate([take(main, e), take(rest, e)[:, :8]], axis=1).astype(BF)
        right = jnp.concatenate([plane_main, plane_rest], axis=1)
        out = jnp.dot(left, right, preferred_element_type=F32)
        low = R * idx
        good = (lane >= low) & (lane < low + R)
        return jnp.concatenate([out[:, :L], jnp.where(good, out[:, L:], 0.0)], axis=1)

    def where_is(q, octant):
        ax, ay = q // 2, lax.rem(q, 2)
        ox, oy, oz = octant // 4, octant // 2 % 2, octant % 2
        return 2 * ax + ox, 2 * ay + oy, oz

    def bits(octant):
        return octant // 4, octant // 2 % 2, octant % 2

    def direct(q):
        for octant in range(8):
            x, y, oz = where_is(q, octant)
            idx = x * 4 + y
            keep[q * 8 + octant] = product(oz * 16 + idx, pz[oz][idx], pz[oz][16], idx)

    def same(k, q):
        axis, shift = (k - 1) // 2, -1 if k % 2 else 1
        for octant in range(8):
            if bits(octant)[axis] != (1 if shift < 0 else 0):
                continue
            x, y, oz = where_is(q, octant)
            near = [x, y, oz]
            near[axis] = near[axis] + shift
            idx = near[0] * 4 + near[1]
            out = product(oz * 16 + x * 4 + y, pz[near[2]][idx], pz[near[2]][16], idx)
            out = out + keep[q * 8 + octant]
            if axis < 2:
                keep[q * 8 + octant] = out
            else:
                e = meta[oz * 16 + x * 4 + y]
                column = pltpu.roll(res_t[...], lax.rem(112 - e + L, L), 1)
                out = jnp.concatenate([out[:, :L], jnp.where(lane == 112, column, out[:, L:])], axis=1)
                x0[q * 8 + octant] = out.astype(BF)

    def outside(k, q):
        axis, shift = (k - 1) // 2, -1 if k % 2 else 1
        ghost = ghosts[k]
        for octant in range(8):
            if bits(octant)[axis] != (0 if shift < 0 else 1):
                continue
            x, y, oz = where_is(q, octant)
            c = oz * 16 + x * 4 + y
            if axis == 2:
                idx = x * 4 + y
                out = product(c, ghost[idx], ghost[16], idx)
                edge = 0 if shift < 0 else 15
                absent = scal[2] * 4 + scal[6] == edge
            else:
                along, other = (x, y) if axis == 0 else (y, x)
                spot = along + shift
                off = (spot < 0) | (spot > 3)
                spot = lax.rem(spot + 4, 4)
                idx = spot * 4 + other if axis == 0 else other * 4 + spot
                plane_main = jnp.where(off, ghost[oz * 4 + other], pz[oz][idx])
                plane_rest = jnp.where(off, ghost[8 + oz], pz[oz][16])
                out = product(c, plane_main, plane_rest, idx)
                edge = 0 if shift < 0 else (1, 3)[axis]
                absent = off & (scal[(3, 5)[axis]] == edge)
            xs[q * 8 + octant] = (out * jnp.where(absent, 0.0, 1.0)).astype(BF)

    def gather(ref, q, octants):
        acc = None
        for octant in octants:
            x, y, oz = where_is(q, octant)
            part = jnp.dot(pt[oz * 16 + x * 4 + y], ref[q * 8 + octant], preferred_element_type=F32)
            acc = part if acc is None else acc + part
        return acc

    def fold(raw, spots, slot):
        total = None
        for spot in spots:
            turned = pltpu.roll(raw, lax.rem(R * slot - R * spot + 2 * L, L), 1)
            total = turned if total is None else total + turned
        good = (lane >= R * slot) & (lane < R * slot + R)
        return jnp.where(good, total, 0.0)

    def finish_sides(axis, q):
        ax, ay = q // 2, lax.rem(q, 2)
        at = meta[E + q]
        remainder = (rem_out if axis == 1 else rem_in)[at]
        for side in range(2):
            acc = gather(xs, q, [o for o in range(8) if bits(o)[axis] == side])
            rows[at, 2 * (axis % 2) + side] = acc[:, :L].astype(BF)
            if axis == 0:
                nx = lax.rem(2 * ax + (-1 if side == 0 else 2) + 4, 4)
                spots = [nx * 4 + 2 * ay + v for v in range(2)]
            elif axis == 1:
                ny = lax.rem(2 * ay + (-1 if side == 0 else 2) + 4, 4)
                spots = [(2 * ax + v) * 4 + ny for v in range(2)]
            else:
                spots = [(2 * ax + v // 2) * 4 + 2 * ay + v % 2 for v in range(4)]
            remainder = remainder + fold(acc[:, L:], spots, 1 + 2 * axis + side)
        if axis == 2:
            rows[at, 2] = remainder.astype(BF)
        else:
            rem_out[at] = remainder

    def finish_centre(q):
        ax, ay = q // 2, lax.rem(q, 2)
        at = meta[E + q]
        acc = gather(x0, q, range(8))
        rows[at, 0] = acc[:, :L].astype(BF)
        raw = acc[:, L:]
        spots = [(2 * ax + v // 2) * 4 + 2 * ay + v % 2 for v in range(4)]
        moved = pltpu.roll(raw, 49 - 112 + L, 1)
        rem_out[at] = jnp.where(lane == 49, moved, fold(raw, spots, 0))

    for i, (k, outer) in enumerate(kinds):
        jac_copy(i).wait()
        spread(lambda row, i=i: jbuf[i % DEPTH, row], main, rest)
        if i + DEPTH < len(kinds):
            jac_copy(i + DEPTH).start()
        if i == 0:
            for copy in early_copies:
                copy.wait()
        if i == 1:
            for copy in late_copies:
                copy.wait()
            if res is not None:
                values = res[...].astype(F32)
                tail = jnp.concatenate([values[:, L:], jnp.zeros((E, L - R), F32)], axis=1)
                res_t[0:L, 0:E] = values[:, :L].T
                res_t[L:H, 0:E] = tail.T[: H - L]

        def run(q, carry, k=k, outer=outer):
            if k == 0:
                direct(q)
            elif outer:
                outside(k, q)
            else:
                same(k, q)
            if outer and k % 2 == 0:
                finish_sides((k - 1) // 2, q)
            if k == 6 and not outer:
                finish_centre(q)
            return carry

        lax.fori_loop(0, 4, run, 0)
    copies = [pltpu.make_async_copy(rows, rows_out, out_sems.at[0])]
    if rem_out is not None:
        copies.append(pltpu.make_async_copy(rem_out, rem_to, out_sems.at[1]))
    for copy in copies:
        copy.start()
    for copy in copies:
        copy.wait()


COMMON = [
    pltpu.VMEM((DEPTH, W, E, W), BF),
    pltpu.VMEM((H * PE, L), F32),
    pltpu.VMEM((H * PE, L), F32),
    pltpu.SemaphoreType.DMA((DEPTH,)),
    pltpu.SemaphoreType.DMA((6,)),
    pltpu.SemaphoreType.DMA((6,)),
    pltpu.SemaphoreType.DMA((2,)),
]
HALF = pltpu.VMEM((E, H, 2 * L), BF)
FULL = pltpu.VMEM((E, H, 2 * L), F32)
REM = pltpu.VMEM((4, H, L), F32)
REST = pltpu.HBM((4, H, L), F32)


def centre_kernel(scal, meta, jac, pz0, pz1, pt, res, rows_out, rem_to, *scratch):
    jbuf, main, rest, j_sems, e_sems, l_sems, o_sems, x0, keep, vz0, vz1, vpt, vres, res_t, rows, rem_out = scratch
    block_kernel(
        [(k, False) for k in range(7)], scal, meta, jac,
        [(pz0, vz0), (pz1, vz1)], [(pt, vpt), (res, vres)],
        ((vz0, vz1), {}, vpt, (vres, res_t), None),
        rows, rows_out.at[:, pl.ds(4, 1)], rem_out, rem_to,
        (jbuf, main, rest, x0, None, keep, j_sems, e_sems, l_sems, o_sems),
    )


def sides_kernel(scal, meta, jac, pz0, pz1, pt, gx, gym, gyp, rem_in, started, rows_out, rem_to, *scratch):
    jbuf, main, rest, j_sems, e_sems, l_sems, o_sems = scratch[:7]
    xs, vz0, vz1, vpt, vx, vym, vyp, vrem, rows, rem_out = scratch[7:]
    block_kernel(
        [(k, True) for k in range(1, 5)], scal, meta, jac,
        [(pz0, vz0), (pz1, vz1), (gx, vx)], [(pt, vpt), (rem_in, vrem), (gym, vym), (gyp, vyp)],
        ((vz0, vz1), {1: vx, 2: vx, 3: vym, 4: vyp}, vpt, (None, None), vrem),
        rows, rows_out.at[:, pl.ds(0, 4)], rem_out, rem_to,
        (jbuf, main, rest, None, xs, None, j_sems, e_sems, l_sems, o_sems),
    )


def depth_kernel(scal, meta, jac, pt, gzm, gzp, rem_in, rows_out, *scratch):
    jbuf, main, rest, j_sems, e_sems, l_sems, o_sems, xs, vpt, vzm, vzp, vrem, rows = scratch
    block_kernel(
        [(k, True) for k in (5, 6)], scal, meta, jac,
        [(gzm, vzm)], [(pt, vpt), (gzp, vzp), (rem_in, vrem)],
        (None, {5: vzm, 6: vzp}, vpt, (None, None), vrem),
        rows, rows_out, None, None,
        (jbuf, main, rest, None, xs, None, j_sems, e_sems, l_sems, o_sems),
    )


def block_call(kernel, operands, out_shape, scratch, name, aliases, cost):
    return pl.pallas_call(
        kernel,
        in_specs=[smem(), smem()] + [anywhere()] * (len(operands) - 2),
        out_specs=[anywhere()] * len(out_shape),
        out_shape=out_shape,
        scratch_shapes=COMMON + scratch,
        input_output_aliases=aliases,
        compiler_params=pltpu.CompilerParams(vmem_limit_bytes=VMEM_LIMIT),
        cost_estimate=pl.CostEstimate(flops=cost, bytes_accessed=1_000_000, transcendentals=0),
        name=name,
    )(*operands)


def final_kernel(scal, *refs):
    held = refs[:10]
    coarse, restricted, out, s1, s2, out_sems = refs[10:]
    lane = lax.broadcasted_iota(jnp.int32, (H, L), 1)

    def plane_of(n, slot):
        part, plane = (0, n) if n < 5 else (1, n - 5)
        z, y = slot // 4, slot % 4
        which, row = [(0, z), (1, z), (3 + z // 2, z % 2), (2, z)][y]
        return held[5 * part + which][row, plane].astype(F32)

    def out_copy(k):
        return pltpu.make_async_copy(out.at[k % 2], coarse.at[k], out_sems.at[k])

    @pl.when(scal[4] == 0)
    def _():
        out[0] = jnp.zeros((W, 16, W), BF)
        restricted[...] = jnp.zeros_like(restricted)
        zero_copies = [pltpu.make_async_copy(out.at[0], coarse.at[k], out_sems.at[k]) for k in range(7)]
        for copy in zero_copies:
            copy.start()
        for copy in zero_copies:
            copy.wait()

    @pl.when(scal[4] == 1)
    def _():
        for k in range(7):
            for slot in range(16):
                s1[pl.ds(slot, H, stride=PS), :] = plane_of([4, 0, 1, 2, 3, 5, 6][k], slot)
                tail = plane_of(7, slot)
                s2[pl.ds(slot, H, stride=PS), :] = pltpu.roll(tail, L - R * k, 1) if k else tail
            if k >= 2:
                out_copy(k - 2).wait()

            def write(i, carry, k=k):
                for u in range(27):
                    row = i * 27 + u
                    at = pl.ds(row * PS, 16)
                    out[k % 2, row] = jnp.concatenate([s1[at, :], s2[at, :R]], axis=1).astype(BF)
                return carry

            lax.fori_loop(0, W // 27, write, 0)
            out_copy(k).start()
        acc = jnp.zeros((H, L), F32)
        for slot in range(16):
            turned = pltpu.roll(plane_of(7, slot), (slot - 49 + L) % L, 1)
            acc = jnp.where(lane == slot, turned, acc)
        restricted[...] = acc.T[:16, :W].astype(BF)
        out_copy(5).wait()
        out_copy(6).wait()


def final_call(scal, rows):
    rows = [pltpu.with_memory_space_constraint(a, pltpu.VMEM) for a in rows]
    return pl.pallas_call(
        final_kernel,
        in_specs=[smem()] + [vmem()] * 10,
        out_specs=[anywhere(), vmem()],
        out_shape=[jax.ShapeDtypeStruct((7, W, 16, W), BF), jax.ShapeDtypeStruct((16, W), BF)],
        scratch_shapes=[
            pltpu.VMEM((2, W, 16, W), BF),
            pltpu.VMEM((H * PS, L), F32),
            pltpu.VMEM((H * PS, L), F32),
            pltpu.SemaphoreType.DMA((7,)),
        ],
        compiler_params=pltpu.CompilerParams(vmem_limit_bytes=VMEM_LIMIT),
        name="assemble",
    )(scal, *rows)


DOWN = [(1, 0), (2, 1), (3, 2), (0, 3)]
UP = [(3, 0), (0, 1), (1, 2), (2, 3)]


def to_owner_row(rows):
    return lax.all_to_all(rows, "zz", split_axis=0, concat_axis=0, tiled=True)


def along_ring(held):
    down = lax.ppermute(held, "yy", DOWN)
    up = lax.ppermute(held, "yy", UP)
    return down, up


def forward(down, up):
    return lax.ppermute(down[:2], "yy", [(1, 0)]), lax.ppermute(up[2:], "yy", [(3, 0)])


def body(jacobian, prolong, residual, neighbours, agg_map, owners):
    gx, gy = lax.axis_index("gx"), lax.axis_index("gy")
    zz, yy = lax.axis_index("zz"), lax.axis_index("yy")
    device = (gx * 4 + gy) * 16 + zz * 4 + yy
    scal = jnp.stack(
        [device * E, device * 4, zz, gx, (yy == 0).astype(jnp.int32), gy, yy]
    ).astype(jnp.int32)
    jac = jnp.transpose(jacobian, (1, 2, 0, 3))
    pro = jnp.transpose(prolong, (1, 0, 2))
    meta, pz0, pz1, xs, ys0, ys1, pt = pack_call(
        scal, stay(neighbours.T), stay(agg_map), stay(owners), pro
    )
    gz = ("zz", "yy")
    ghost_x = lax.ppermute(xs, "gx", [(0, 1), (1, 0)])
    ghost_zm = lax.ppermute(pz1, gz, [(i, (i + 1) % 16) for i in range(16)])
    ghost_zp = lax.ppermute(pz0, gz, [((i + 1) % 16, i) for i in range(16)])
    ghost_ym = lax.ppermute(ys1, "gy", [(i, (i + 1) % 4) for i in range(4)])
    ghost_yp = lax.ppermute(ys0, "gy", [((i + 1) % 4, i) for i in range(4)])
    five = jax.ShapeDtypeStruct((4, 5, H, L), BF)
    z_face, side_face = [pltpu.VMEM((n, H, L), BF) for n in (17, 10)]
    turned = pltpu.VMEM((E, H, H), BF)
    first, rem = block_call(
        centre_kernel, (scal, meta, jac, pz0, pz1, pt, stay(residual)), [five, REST],
        [HALF, FULL, z_face, z_face, turned, pltpu.VMEM((E, W), BF), pltpu.VMEM((H, L), F32), pltpu.VMEM((4, 1, H, L), BF), REM],
        "centre", {}, 18_000_000_000,
    )
    first, rem = block_call(
        sides_kernel, (scal, meta, jac, pz0, pz1, pt, ghost_x, ghost_ym, ghost_yp, stay(rem), first), [five, REST],
        [HALF, z_face, z_face, turned, side_face, side_face, side_face, REM, pltpu.VMEM((4, 4, H, L), BF), REM],
        "sides", {10: 0}, 12_000_000_000,
    )
    held1 = to_owner_row(first)
    (second,) = block_call(
        depth_kernel, (scal, meta, jac, pt, ghost_zm, ghost_zp, stay(rem)),
        [jax.ShapeDtypeStruct((4, 3, H, L), BF)],
        [HALF, turned, z_face, z_face, REM, pltpu.VMEM((4, 3, H, L), BF)],
        "depth", {}, 9_000_000_000,
    )
    held1, second = lax.optimization_barrier((held1, second))
    down1, up1 = along_ring(held1)
    held2 = to_owner_row(second)
    twice1 = forward(down1, up1)
    down2, up2 = along_ring(held2)
    twice2 = forward(down2, up2)
    coarse, restricted = final_call(scal, (held1, down1, up1) + twice1 + (held2, down2, up2) + twice2)
    return jnp.transpose(coarse, (2, 0, 1, 3)), restricted


def solution(mesh):
    fine = Mesh(mesh.devices.reshape(2, 4, 4, 4), ("gx", "gy", "zz", "yy"))
    every = ("gx", "gy", "zz", "yy")
    return jax.shard_map(
        body,
        mesh=fine,
        in_specs=(P(every), P(every), P(every), P(every), P(every), P(every)),
        out_specs=(P(every), P(every)),
        check_vma=False,
    )
```

```python
import functools

import jax
import jax.numpy as jnp
from jax import lax
from jax.experimental import pallas as pl
from jax.experimental.pallas import tpu as pltpu
from jax.sharding import Mesh, PartitionSpec as P

E = 32
W = 135
H = 136
L = 128
R = W - L
PE = 36
PS = 20
BF = jnp.bfloat16
F32 = jnp.float32
VMEM_LIMIT = 40 * 1024 * 1024
PACK_LIMIT = 40 * 1024 * 1024


def anywhere():
    return pl.BlockSpec(memory_space=pl.ANY)


def stay(array):
    return pltpu.with_memory_space_constraint(array, pltpu.HBM)


def smem():
    return pl.BlockSpec(memory_space=pltpu.SMEM)


def vmem():
    return pl.BlockSpec(memory_space=pltpu.VMEM)


def spread(block, main, rest, base=0, count=W):
    def step(i, carry):
        for u in range(9):
            row = base + i * 9 + u
            values = block(row).astype(F32)
            at = pl.ds(row * PE, E)
            main[at, :] = values[:, :L]
            rest[at, 0:R] = values[:, L:]
        return carry

    lax.fori_loop(0, count // 9, step, 0)


def clear(main, rest):
    main[W * PE : H * PE, :] = jnp.zeros((PE, L), F32)
    rest[...] = jnp.zeros((H * PE, L), F32)


def take(ref, element):
    return ref[pl.ds(element, H, stride=PE), :]


def pack_kernel(
    scal, nbr_in, agg_in, own_in, p_in, meta, pz0_out, pz1_out, xs_out, ys0_out, ys1_out, pt_out,
    main, rest, nbr, agg, own, p_ref, pz0, pz1, xs, ys0, ys1, pt, sems, p_sems, out_sems,
):
    pz, ys = (pz0, pz1), (ys0, ys1)
    chunk = W // 5
    p_copies = [
        pltpu.make_async_copy(
            p_in.at[pl.ds(i * chunk, chunk)], p_ref.at[pl.ds(i * chunk, chunk)], p_sems.at[i]
        )
        for i in range(5)
    ]
    for copy in p_copies:
        copy.start()
    out_copies = [
        pltpu.make_async_copy(a, b, out_sems.at[i])
        for i, (a, b) in enumerate(
            [
                (pz0, pz0_out),
                (pt.at[pl.ds(0, 16)], pt_out.at[pl.ds(0, 16)]),
                (pz1, pz1_out),
                (pt.at[pl.ds(16, 16)], pt_out.at[pl.ds(16, 16)]),
                (xs, xs_out),
                (ys0, ys0_out),
                (ys1, ys1_out),
            ]
        )
    ]
    base = scal[0]
    copies = [
        pltpu.make_async_copy(a, b, sems.at[i])
        for i, (a, b) in enumerate([(nbr_in, nbr), (agg_in, agg), (own_in, own)])
    ]
    for copy in copies:
        copy.start()
    clear(main, rest)
    for i in range(5):
        p_copies[i].wait()
        spread(lambda row: p_ref[row], main, rest, i * chunk, chunk)
    for copy in copies:
        copy.wait()

    def place(e, carry):
        def near(direction):
            local = nbr[direction, e] - base
            here = (local >= 0) & (local < E)
            safe = jnp.clip(local, 0, E - 1)
            same = here & (agg[safe] == agg[e])
            return here.astype(jnp.int32), same.astype(jnp.int32)

        here_xm, odd_x = near(0)
        here_xp, _ = near(1)
        here_ym, odd_y = near(2)
        here_yp, _ = near(3)
        _, odd_z = near(4)
        agg_x = jnp.where(odd_x == 1, 1 - here_xp, here_xm)
        agg_y = jnp.where(odd_y == 1, 1 - here_yp, here_ym)
        meta[odd_z * 16 + (2 * agg_x + odd_x) * 4 + 2 * agg_y + odd_y] = e
        owner = own[agg[e] - scal[1]]
        meta[E + agg_x * 2 + agg_y] = owner // 4
        return carry

    lax.fori_loop(0, E, place, 0)
    for oz in range(2):
        plane = jnp.zeros((H, L), F32)
        for xy in range(16):
            e = meta[oz * 16 + xy]
            a = take(main, e)
            b = take(rest, e)
            pz[oz][xy] = a.astype(BF)
            plane = plane + (pltpu.roll(b, R * xy, 1) if xy else b)
            pt[oz * 16 + xy] = jnp.concatenate([a.T, b.T[:8]], axis=0).astype(BF)
        pz[oz][16] = plane.astype(BF)
        out_copies[2 * oz].start()
        out_copies[2 * oz + 1].start()
    face = jnp.where(scal[3] == 0, 12, 0)
    for oz in range(2):
        for v in range(4):
            xs[oz * 4 + v] = pz[oz][face + v]
            ys[0][oz * 4 + v] = pz[oz][v * 4]
            ys[1][oz * 4 + v] = pz[oz][v * 4 + 3]
        xs[8 + oz] = pz[oz][16]
        ys[0][8 + oz] = pz[oz][16]
        ys[1][8 + oz] = pz[oz][16]
    for copy in out_copies[4:]:
        copy.start()
    for copy in out_copies:
        copy.wait()


def pack_call(*operands):
    return pl.pallas_call(
        pack_kernel,
        in_specs=[smem()] + [anywhere()] * 4,
        out_specs=[smem()] + [anywhere()] * 6,
        out_shape=[
            jax.ShapeDtypeStruct((40,), jnp.int32),
            jax.ShapeDtypeStruct((17, H, L), BF),
            jax.ShapeDtypeStruct((17, H, L), BF),
            jax.ShapeDtypeStruct((10, H, L), BF),
            jax.ShapeDtypeStruct((10, H, L), BF),
            jax.ShapeDtypeStruct((10, H, L), BF),
            jax.ShapeDtypeStruct((E, H, H), BF),
        ],
        scratch_shapes=[
            pltpu.VMEM((H * PE, L), F32),
            pltpu.VMEM((H * PE, L), F32),
            pltpu.SMEM((6, E), jnp.int32),
            pltpu.SMEM((E,), jnp.int32),
            pltpu.SMEM((4,), jnp.int32),
            pltpu.VMEM((W, E, W), BF),
            pltpu.VMEM((17, H, L), BF),
            pltpu.VMEM((17, H, L), BF),
            pltpu.VMEM((10, H, L), BF),
            pltpu.VMEM((10, H, L), BF),
            pltpu.VMEM((10, H, L), BF),
            pltpu.VMEM((E, H, H), BF),
            pltpu.SemaphoreType.DMA((3,)),
            pltpu.SemaphoreType.DMA((5,)),
            pltpu.SemaphoreType.DMA((7,)),
        ],
        compiler_params=pltpu.CompilerParams(vmem_limit_bytes=PACK_LIMIT),
        name="pack",
    )(*operands)


DEPTH = 3


def block_kernel(kinds, scal, meta, jac, early, late, views, rows, rows_out, rem_out, rem_to, buffers):
    jbuf, main, rest, x0, xs, keep, jac_sems, early_sems, late_sems, out_sems = buffers
    pz, ghosts, pt, (res, res_t), rem_in = views
    lane = lax.broadcasted_iota(jnp.int32, (H, L), 1)

    def jac_copy(i):
        return pltpu.make_async_copy(jac.at[kinds[i][0]], jbuf.at[i % DEPTH], jac_sems.at[i % DEPTH])

    early_copies = [pltpu.make_async_copy(a, b, early_sems.at[i]) for i, (a, b) in enumerate(early)]
    late_copies = [pltpu.make_async_copy(a, b, late_sems.at[i]) for i, (a, b) in enumerate(late)]
    jac_copy(0).start()
    for copy in early_copies:
        copy.start()
    jac_copy(1).start()
    for copy in late_copies:
        copy.start()
    if len(kinds) > 2:
        jac_copy(2).start()
    clear(main, rest)

    def product(c, plane_main, plane_rest, idx):
        e = meta[c]
        left = jnp.concatenate([take(main, e), take(rest, e)[:, :8]], axis=1).astype(BF)
        right = jnp.concatenate([plane_main, plane_rest], axis=1)
        out = jnp.dot(left, right, preferred_element_type=F32)
        low = R * idx
        good = (lane >= low) & (lane < low + R)
        return jnp.concatenate([out[:, :L], jnp.where(good, out[:, L:], 0.0)], axis=1)

    def where_is(q, octant):
        ax, ay = q // 2, lax.rem(q, 2)
        ox, oy, oz = octant // 4, octant // 2 % 2, octant % 2
        return 2 * ax + ox, 2 * ay + oy, oz

    def bits(octant):
        return octant // 4, octant // 2 % 2, octant % 2

    def direct(q):
        for octant in range(8):
            x, y, oz = where_is(q, octant)
            idx = x * 4 + y
            keep[q * 8 + octant] = product(oz * 16 + idx, pz[oz][idx], pz[oz][16], idx)

    def same(k, q):
        axis, shift = (k - 1) // 2, -1 if k % 2 else 1
        for octant in range(8):
            if bits(octant)[axis] != (1 if shift < 0 else 0):
                continue
            x, y, oz = where_is(q, octant)
            near = [x, y, oz]
            near[axis] = near[axis] + shift
            idx = near[0] * 4 + near[1]
            out = product(oz * 16 + x * 4 + y, pz[near[2]][idx], pz[near[2]][16], idx)
            out = out + keep[q * 8 + octant]
            if axis < 2:
                keep[q * 8 + octant] = out
            else:
                e = meta[oz * 16 + x * 4 + y]
                column = pltpu.roll(res_t[...], lax.rem(112 - e + L, L), 1)
                out = jnp.concatenate([out[:, :L], jnp.where(lane == 112, column, out[:, L:])], axis=1)
                x0[q * 8 + octant] = out.astype(BF)

    def outside(k, q):
        axis, shift = (k - 1) // 2, -1 if k % 2 else 1
        ghost = ghosts[k]
        for octant in range(8):
            if bits(octant)[axis] != (0 if shift < 0 else 1):
                continue
            x, y, oz = where_is(q, octant)
            c = oz * 16 + x * 4 + y
            if axis == 2:
                idx = x * 4 + y
                out = product(c, ghost[idx], ghost[16], idx)
                edge = 0 if shift < 0 else 15
                absent = scal[2] * 4 + scal[6] == edge
            else:
                along, other = (x, y) if axis == 0 else (y, x)
                spot = along + shift
                off = (spot < 0) | (spot > 3)
                spot = lax.rem(spot + 4, 4)
                idx = spot * 4 + other if axis == 0 else other * 4 + spot
                plane_main = jnp.where(off, ghost[oz * 4 + other], pz[oz][idx])
                plane_rest = jnp.where(off, ghost[8 + oz], pz[oz][16])
                out = product(c, plane_main, plane_rest, idx)
                edge = 0 if shift < 0 else (1, 3)[axis]
                absent = off & (scal[(3, 5)[axis]] == edge)
            xs[q * 8 + octant] = (out * jnp.where(absent, 0.0, 1.0)).astype(BF)

    def gather(ref, q, octants):
        acc = None
        for octant in octants:
            x, y, oz = where_is(q, octant)
            part = jnp.dot(pt[oz * 16 + x * 4 + y], ref[q * 8 + octant], preferred_element_type=F32)
            acc = part if acc is None else acc + part
        return acc

    def fold(raw, spots, slot):
        total = None
        for spot in spots:
            turned = pltpu.roll(raw, lax.rem(R * slot - R * spot + 2 * L, L), 1)
            total = turned if total is None else total + turned
        good = (lane >= R * slot) & (lane < R * slot + R)
        return jnp.where(good, total, 0.0)

    def finish_sides(axis, q):
        ax, ay = q // 2, lax.rem(q, 2)
        at = meta[E + q]
        remainder = (rem_out if axis == 1 else rem_in)[at]
        for side in range(2):
            acc = gather(xs, q, [o for o in range(8) if bits(o)[axis] == side])
            rows[at, 2 * (axis % 2) + side] = acc[:, :L].astype(BF)
            if axis == 0:
                nx = lax.rem(2 * ax + (-1 if side == 0 else 2) + 4, 4)
                spots = [nx * 4 + 2 * ay + v for v in range(2)]
            elif axis == 1:
                ny = lax.rem(2 * ay + (-1 if side == 0 else 2) + 4, 4)
                spots = [(2 * ax + v) * 4 + ny for v in range(2)]
            else:
                spots = [(2 * ax + v // 2) * 4 + 2 * ay + v % 2 for v in range(4)]
            remainder = remainder + fold(acc[:, L:], spots, 1 + 2 * axis + side)
        if axis == 2:
            rows[at, 2] = remainder.astype(BF)
        else:
            rem_out[at] = remainder

    def finish_centre(q):
        ax, ay = q // 2, lax.rem(q, 2)
        at = meta[E + q]
        acc = gather(x0, q, range(8))
        rows[at, 0] = acc[:, :L].astype(BF)
        raw = acc[:, L:]
        spots = [(2 * ax + v // 2) * 4 + 2 * ay + v % 2 for v in range(4)]
        moved = pltpu.roll(raw, 49 - 112 + L, 1)
        rem_out[at] = jnp.where(lane == 49, moved, fold(raw, spots, 0))

    for i, (k, outer) in enumerate(kinds):
        jac_copy(i).wait()
        spread(lambda row, i=i: jbuf[i % DEPTH, row], main, rest)
        if i + DEPTH < len(kinds):
            jac_copy(i + DEPTH).start()
        if i == 0:
            for copy in early_copies:
                copy.wait()
        if i == 1:
            for copy in late_copies:
                copy.wait()
            if res is not None:
                values = res[...].astype(F32)
                tail = jnp.concatenate([values[:, L:], jnp.zeros((E, L - R), F32)], axis=1)
                res_t[0:L, 0:E] = values[:, :L].T
                res_t[L:H, 0:E] = tail.T[: H - L]

        def run(q, carry, k=k, outer=outer):
            if k == 0:
                direct(q)
            elif outer:
                outside(k, q)
            else:
                same(k, q)
            if outer and k % 2 == 0:
                finish_sides((k - 1) // 2, q)
            if k == 6 and not outer:
                finish_centre(q)
            return carry

        lax.fori_loop(0, 4, run, 0)
    copies = [pltpu.make_async_copy(rows, rows_out, out_sems.at[0])]
    if rem_out is not None:
        copies.append(pltpu.make_async_copy(rem_out, rem_to, out_sems.at[1]))
    for copy in copies:
        copy.start()
    for copy in copies:
        copy.wait()


COMMON = [
    pltpu.VMEM((DEPTH, W, E, W), BF),
    pltpu.VMEM((H * PE, L), F32),
    pltpu.VMEM((H * PE, L), F32),
    pltpu.SemaphoreType.DMA((DEPTH,)),
    pltpu.SemaphoreType.DMA((6,)),
    pltpu.SemaphoreType.DMA((6,)),
    pltpu.SemaphoreType.DMA((2,)),
]
HALF = pltpu.VMEM((E, H, 2 * L), BF)
FULL = pltpu.VMEM((E, H, 2 * L), F32)
REM = pltpu.VMEM((4, H, L), F32)
REST = pltpu.HBM((4, H, L), F32)


def centre_kernel(scal, meta, jac, pz0, pz1, pt, res, rows_out, rem_to, *scratch):
    jbuf, main, rest, j_sems, e_sems, l_sems, o_sems, x0, keep, vz0, vz1, vpt, vres, res_t, rows, rem_out = scratch
    block_kernel(
        [(k, False) for k in range(7)], scal, meta, jac,
        [(pz0, vz0), (pz1, vz1)], [(pt, vpt), (res, vres)],
        ((vz0, vz1), {}, vpt, (vres, res_t), None),
        rows, rows_out.at[:, pl.ds(4, 1)], rem_out, rem_to,
        (jbuf, main, rest, x0, None, keep, j_sems, e_sems, l_sems, o_sems),
    )


def sides_kernel(scal, meta, jac, pz0, pz1, pt, gx, gym, gyp, rem_in, started, rows_out, rem_to, *scratch):
    jbuf, main, rest, j_sems, e_sems, l_sems, o_sems = scratch[:7]
    xs, vz0, vz1, vpt, vx, vym, vyp, vrem, rows, rem_out = scratch[7:]
    block_kernel(
        [(k, True) for k in range(1, 5)], scal, meta, jac,
        [(pz0, vz0), (pz1, vz1), (gx, vx)], [(pt, vpt), (rem_in, vrem), (gym, vym), (gyp, vyp)],
        ((vz0, vz1), {1: vx, 2: vx, 3: vym, 4: vyp}, vpt, (None, None), vrem),
        rows, rows_out.at[:, pl.ds(0, 4)], rem_out, rem_to,
        (jbuf, main, rest, None, xs, None, j_sems, e_sems, l_sems, o_sems),
    )


def depth_kernel(scal, meta, jac, pt, gzm, gzp, rem_in, rows_out, *scratch):
    jbuf, main, rest, j_sems, e_sems, l_sems, o_sems, xs, vpt, vzm, vzp, vrem, rows = scratch
    block_kernel(
        [(k, True) for k in (5, 6)], scal, meta, jac,
        [(gzm, vzm)], [(pt, vpt), (gzp, vzp), (rem_in, vrem)],
        (None, {5: vzm, 6: vzp}, vpt, (None, None), vrem),
        rows, rows_out, None, None,
        (jbuf, main, rest, None, xs, None, j_sems, e_sems, l_sems, o_sems),
    )


def block_call(kernel, operands, out_shape, scratch, name, aliases, cost):
    return pl.pallas_call(
        kernel,
        in_specs=[smem(), smem()] + [anywhere()] * (len(operands) - 2),
        out_specs=[anywhere()] * len(out_shape),
        out_shape=out_shape,
        scratch_shapes=COMMON + scratch,
        input_output_aliases=aliases,
        compiler_params=pltpu.CompilerParams(vmem_limit_bytes=VMEM_LIMIT),
        cost_estimate=pl.CostEstimate(flops=cost, bytes_accessed=1_000_000, transcendentals=0),
        name=name,
    )(*operands)


def final_kernel(scal, *refs):
    held = refs[:10]
    coarse, restricted, out, s1, s2, out_sems = refs[10:]
    lane = lax.broadcasted_iota(jnp.int32, (H, L), 1)

    def plane_of(n, slot):
        part, plane = (0, n) if n < 5 else (1, n - 5)
        z, y = slot // 4, slot % 4
        which, row = [(0, z), (1, z), (3 + z // 2, z % 2), (2, z)][y]
        return held[5 * part + which][row, plane].astype(F32)

    def out_copy(k):
        return pltpu.make_async_copy(out.at[k % 2], coarse.at[k], out_sems.at[k])

    @pl.when(scal[4] == 0)
    def _():
        out[0] = jnp.zeros((W, 16, W), BF)
        restricted[...] = jnp.zeros_like(restricted)
        zero_copies = [pltpu.make_async_copy(out.at[0], coarse.at[k], out_sems.at[k]) for k in range(7)]
        for copy in zero_copies:
            copy.start()
        for copy in zero_copies:
            copy.wait()

    @pl.when(scal[4] == 1)
    def _():
        for k in range(7):
            for slot in range(16):
                s1[pl.ds(slot, H, stride=PS), :] = plane_of([4, 0, 1, 2, 3, 5, 6][k], slot)
                tail = plane_of(7, slot)
                s2[pl.ds(slot, H, stride=PS), :] = pltpu.roll(tail, L - R * k, 1) if k else tail
            if k >= 2:
                out_copy(k - 2).wait()

            def write(i, carry, k=k):
                for u in range(27):
                    row = i * 27 + u
                    at = pl.ds(row * PS, 16)
                    out[k % 2, row] = jnp.concatenate([s1[at, :], s2[at, :R]], axis=1).astype(BF)
                return carry

            lax.fori_loop(0, W // 27, write, 0)
            out_copy(k).start()
        acc = jnp.zeros((H, L), F32)
        for slot in range(16):
            turned = pltpu.roll(plane_of(7, slot), (slot - 49 + L) % L, 1)
            acc = jnp.where(lane == slot, turned, acc)
        restricted[...] = acc.T[:16, :W].astype(BF)
        out_copy(5).wait()
        out_copy(6).wait()


def final_call(scal, rows):
    rows = [pltpu.with_memory_space_constraint(a, pltpu.VMEM) for a in rows]
    return pl.pallas_call(
        final_kernel,
        in_specs=[smem()] + [vmem()] * 10,
        out_specs=[anywhere(), vmem()],
        out_shape=[jax.ShapeDtypeStruct((7, W, 16, W), BF), jax.ShapeDtypeStruct((16, W), BF)],
        scratch_shapes=[
            pltpu.VMEM((2, W, 16, W), BF),
            pltpu.VMEM((H * PS, L), F32),
            pltpu.VMEM((H * PS, L), F32),
            pltpu.SemaphoreType.DMA((7,)),
        ],
        compiler_params=pltpu.CompilerParams(vmem_limit_bytes=VMEM_LIMIT),
        name="assemble",
    )(scal, *rows)


DOWN = [(1, 0), (2, 1), (3, 2), (0, 3)]
UP = [(3, 0), (0, 1), (1, 2), (2, 3)]


def to_owner_row(rows):
    return lax.all_to_all(rows, "zz", split_axis=0, concat_axis=0, tiled=True)


def along_ring(held):
    down = lax.ppermute(held, "yy", DOWN)
    up = lax.ppermute(held, "yy", UP)
    return down, up


def forward(down, up):
    return lax.ppermute(down[:2], "yy", [(1, 0)]), lax.ppermute(up[2:], "yy", [(3, 0)])


def body(jacobian, prolong, residual, neighbours, agg_map, owners):
    gx, gy = lax.axis_index("gx"), lax.axis_index("gy")
    zz, yy = lax.axis_index("zz"), lax.axis_index("yy")
    device = (gx * 4 + gy) * 16 + zz * 4 + yy
    scal = jnp.stack(
        [device * E, device * 4, zz, gx, (yy == 0).astype(jnp.int32), gy, yy]
    ).astype(jnp.int32)
    jac = jnp.transpose(jacobian, (1, 2, 0, 3))
    pro = jnp.transpose(prolong, (1, 0, 2))
    meta, pz0, pz1, xs, ys0, ys1, pt = pack_call(
        scal, stay(neighbours.T), stay(agg_map), stay(owners), stay(pro)
    )
    gz = ("zz", "yy")
    ghost_x = lax.ppermute(xs, "gx", [(0, 1), (1, 0)])
    ghost_zm = lax.ppermute(pz1, gz, [(i, (i + 1) % 16) for i in range(16)])
    ghost_zp = lax.ppermute(pz0, gz, [((i + 1) % 16, i) for i in range(16)])
    ghost_ym = lax.ppermute(ys1, "gy", [(i, (i + 1) % 4) for i in range(4)])
    ghost_yp = lax.ppermute(ys0, "gy", [((i + 1) % 4, i) for i in range(4)])
    five = jax.ShapeDtypeStruct((4, 5, H, L), BF)
    z_face, side_face = [pltpu.VMEM((n, H, L), BF) for n in (17, 10)]
    turned = pltpu.VMEM((E, H, H), BF)
    first, rem = block_call(
        centre_kernel, (scal, meta, jac, pz0, pz1, pt, stay(residual)), [five, REST],
        [HALF, FULL, z_face, z_face, turned, pltpu.VMEM((E, W), BF), pltpu.VMEM((H, L), F32), pltpu.VMEM((4, 1, H, L), BF), REM],
        "centre", {}, 18_000_000_000,
    )
    first, rem = block_call(
        sides_kernel, (scal, meta, jac, pz0, pz1, pt, ghost_x, ghost_ym, ghost_yp, stay(rem), first), [five, REST],
        [HALF, z_face, z_face, turned, side_face, side_face, side_face, REM, pltpu.VMEM((4, 4, H, L), BF), REM],
        "sides", {10: 0}, 12_000_000_000,
    )
    held1 = to_owner_row(first)
    (second,) = block_call(
        depth_kernel, (scal, meta, jac, pt, ghost_zm, ghost_zp, stay(rem)),
        [jax.ShapeDtypeStruct((4, 3, H, L), BF)],
        [HALF, turned, z_face, z_face, REM, pltpu.VMEM((4, 3, H, L), BF)],
        "depth", {}, 9_000_000_000,
    )
    held1, second = lax.optimization_barrier((held1, second))
    down1, up1 = along_ring(held1)
    held2 = to_owner_row(second)
    twice1 = forward(down1, up1)
    down2, up2 = along_ring(held2)
    twice2 = forward(down2, up2)
    coarse, restricted = final_call(scal, (held1, down1, up1) + twice1 + (held2, down2, up2) + twice2)
    return jnp.transpose(coarse, (2, 0, 1, 3)), restricted


def solution(mesh):
    fine = Mesh(mesh.devices.reshape(2, 4, 4, 4), ("gx", "gy", "zz", "yy"))
    every = ("gx", "gy", "zz", "yy")
    return jax.shard_map(
        body,
        mesh=fine,
        in_specs=(P(every), P(every), P(every), P(every), P(every), P(every)),
        out_specs=(P(every), P(every)),
        check_vma=False,
    )
```

```python
import functools

import jax
import jax.numpy as jnp
from jax import lax
from jax.experimental import pallas as pl
from jax.experimental.pallas import tpu as pltpu
from jax.sharding import Mesh, PartitionSpec as P

E = 32
W = 135
H = 136
L = 128
R = W - L
PE = 36
PS = 20
BF = jnp.bfloat16
F32 = jnp.float32
VMEM_LIMIT = 40 * 1024 * 1024
PACK_LIMIT = 40 * 1024 * 1024


def anywhere():
    return pl.BlockSpec(memory_space=pl.ANY)


def stay(array):
    return pltpu.with_memory_space_constraint(array, pltpu.HBM)


def smem():
    return pl.BlockSpec(memory_space=pltpu.SMEM)


def vmem():
    return pl.BlockSpec(memory_space=pltpu.VMEM)


def spread(block, main, rest, base=0, count=W):
    def step(i, carry):
        for u in range(9):
            row = base + i * 9 + u
            values = block(row).astype(F32)
            at = pl.ds(row * PE, E)
            main[at, :] = values[:, :L]
            rest[at, 0:R] = values[:, L:]
        return carry

    lax.fori_loop(0, count // 9, step, 0)


def clear(main, rest):
    main[W * PE : H * PE, :] = jnp.zeros((PE, L), F32)
    rest[...] = jnp.zeros((H * PE, L), F32)


def take(ref, element):
    return ref[pl.ds(element, H, stride=PE), :]


def pack_kernel(
    scal, nbr_in, agg_in, own_in, p_in, meta, pz0_out, pz1_out, xs_out, ys0_out, ys1_out, pt_out,
    main, rest, nbr, agg, own, p_ref, pz0, pz1, xs, ys0, ys1, pt, sems, p_sems, out_sems,
):
    pz, ys = (pz0, pz1), (ys0, ys1)
    chunk = W // 5
    p_copies = [
        pltpu.make_async_copy(
            p_in.at[pl.ds(i * chunk, chunk)], p_ref.at[pl.ds(i * chunk, chunk)], p_sems.at[i]
        )
        for i in range(5)
    ]
    for copy in p_copies:
        copy.start()
    out_copies = [
        pltpu.make_async_copy(a, b, out_sems.at[i])
        for i, (a, b) in enumerate(
            [
                (pz0, pz0_out),
                (pt.at[pl.ds(0, 16)], pt_out.at[pl.ds(0, 16)]),
                (pz1, pz1_out),
                (pt.at[pl.ds(16, 16)], pt_out.at[pl.ds(16, 16)]),
                (xs, xs_out),
                (ys0, ys0_out),
                (ys1, ys1_out),
            ]
        )
    ]
    base = scal[0]
    copies = [
        pltpu.make_async_copy(a, b, sems.at[i])
        for i, (a, b) in enumerate([(nbr_in, nbr), (agg_in, agg), (own_in, own)])
    ]
    for copy in copies:
        copy.start()
    clear(main, rest)
    for i in range(5):
        p_copies[i].wait()
        spread(lambda row: p_ref[row], main, rest, i * chunk, chunk)
    for copy in copies:
        copy.wait()

    def place(e, carry):
        def near(direction):
            local = nbr[direction, e] - base
            here = (local >= 0) & (local < E)
            safe = jnp.clip(local, 0, E - 1)
            same = here & (agg[safe] == agg[e])
            return here.astype(jnp.int32), same.astype(jnp.int32)

        here_xm, odd_x = near(0)
        here_xp, _ = near(1)
        here_ym, odd_y = near(2)
        here_yp, _ = near(3)
        _, odd_z = near(4)
        agg_x = jnp.where(odd_x == 1, 1 - here_xp, here_xm)
        agg_y = jnp.where(odd_y == 1, 1 - here_yp, here_ym)
        meta[odd_z * 16 + (2 * agg_x + odd_x) * 4 + 2 * agg_y + odd_y] = e
        owner = own[agg[e] - scal[1]]
        meta[E + agg_x * 2 + agg_y] = owner // 4
        return carry

    lax.fori_loop(0, E, place, 0)
    for oz in range(2):
        plane = jnp.zeros((H, L), F32)
        for xy in range(16):
            e = meta[oz * 16 + xy]
            a = take(main, e)
            b = take(rest, e)
            pz[oz][xy] = a.astype(BF)
            plane = plane + (pltpu.roll(b, R * xy, 1) if xy else b)
            pt[oz * 16 + xy] = jnp.concatenate([a.T, b.T[:8]], axis=0).astype(BF)
        pz[oz][16] = plane.astype(BF)
        out_copies[2 * oz].start()
        out_copies[2 * oz + 1].start()
    face = jnp.where(scal[3] == 0, 12, 0)
    for oz in range(2):
        for v in range(4):
            xs[oz * 4 + v] = pz[oz][face + v]
            ys[0][oz * 4 + v] = pz[oz][v * 4]
            ys[1][oz * 4 + v] = pz[oz][v * 4 + 3]
        xs[8 + oz] = pz[oz][16]
        ys[0][8 + oz] = pz[oz][16]
        ys[1][8 + oz] = pz[oz][16]
    for copy in out_copies[4:]:
        copy.start()
    for copy in out_copies:
        copy.wait()


def pack_call(*operands):
    return pl.pallas_call(
        pack_kernel,
        in_specs=[smem()] + [anywhere()] * 4,
        out_specs=[smem()] + [anywhere()] * 6,
        out_shape=[
            jax.ShapeDtypeStruct((40,), jnp.int32),
            jax.ShapeDtypeStruct((17, H, L), BF),
            jax.ShapeDtypeStruct((17, H, L), BF),
            jax.ShapeDtypeStruct((10, H, L), BF),
            jax.ShapeDtypeStruct((10, H, L), BF),
            jax.ShapeDtypeStruct((10, H, L), BF),
            jax.ShapeDtypeStruct((E, H, H), BF),
        ],
        scratch_shapes=[
            pltpu.VMEM((H * PE, L), F32),
            pltpu.VMEM((H * PE, L), F32),
            pltpu.SMEM((6, E), jnp.int32),
            pltpu.SMEM((E,), jnp.int32),
            pltpu.SMEM((4,), jnp.int32),
            pltpu.VMEM((W, E, W), BF),
            pltpu.VMEM((17, H, L), BF),
            pltpu.VMEM((17, H, L), BF),
            pltpu.VMEM((10, H, L), BF),
            pltpu.VMEM((10, H, L), BF),
            pltpu.VMEM((10, H, L), BF),
            pltpu.VMEM((E, H, H), BF),
            pltpu.SemaphoreType.DMA((3,)),
            pltpu.SemaphoreType.DMA((5,)),
            pltpu.SemaphoreType.DMA((7,)),
        ],
        compiler_params=pltpu.CompilerParams(vmem_limit_bytes=PACK_LIMIT),
        name="pack",
    )(*operands)


DEPTH = 3


def block_kernel(kinds, scal, meta, jac, early, late, views, rows, rows_out, rem_out, rem_to, buffers):
    jbuf, main, rest, x0, xs, keep, jac_sems, early_sems, late_sems, out_sems = buffers
    pz, ghosts, pt, (res, res_t), rem_in = views
    lane = lax.broadcasted_iota(jnp.int32, (H, L), 1)

    def jac_copy(i):
        return pltpu.make_async_copy(jac.at[kinds[i][0]], jbuf.at[i % DEPTH], jac_sems.at[i % DEPTH])

    early_copies = [pltpu.make_async_copy(a, b, early_sems.at[i]) for i, (a, b) in enumerate(early)]
    late_copies = [pltpu.make_async_copy(a, b, late_sems.at[i]) for i, (a, b) in enumerate(late)]
    jac_copy(0).start()
    for copy in early_copies:
        copy.start()
    jac_copy(1).start()
    for copy in late_copies:
        copy.start()
    if len(kinds) > 2:
        jac_copy(2).start()
    clear(main, rest)

    def product(c, plane_main, plane_rest, idx):
        e = meta[c]
        left = jnp.concatenate([take(main, e), take(rest, e)[:, :8]], axis=1).astype(BF)
        right = jnp.concatenate([plane_main, plane_rest], axis=1)
        out = jnp.dot(left, right, preferred_element_type=F32)
        low = R * idx
        good = (lane >= low) & (lane < low + R)
        return jnp.concatenate([out[:, :L], jnp.where(good, out[:, L:], 0.0)], axis=1)

    def where_is(q, octant):
        ax, ay = q // 2, lax.rem(q, 2)
        ox, oy, oz = octant // 4, octant // 2 % 2, octant % 2
        return 2 * ax + ox, 2 * ay + oy, oz

    def bits(octant):
        return octant // 4, octant // 2 % 2, octant % 2

    def direct(q):
        for octant in range(8):
            x, y, oz = where_is(q, octant)
            idx = x * 4 + y
            keep[q * 8 + octant] = product(oz * 16 + idx, pz[oz][idx], pz[oz][16], idx)

    def same(k, q):
        axis, shift = (k - 1) // 2, -1 if k % 2 else 1
        for octant in range(8):
            if bits(octant)[axis] != (1 if shift < 0 else 0):
                continue
            x, y, oz = where_is(q, octant)
            near = [x, y, oz]
            near[axis] = near[axis] + shift
            idx = near[0] * 4 + near[1]
            out = product(oz * 16 + x * 4 + y, pz[near[2]][idx], pz[near[2]][16], idx)
            out = out + keep[q * 8 + octant]
            if axis < 2:
                keep[q * 8 + octant] = out
            else:
                e = meta[oz * 16 + x * 4 + y]
                column = pltpu.roll(res_t[...], lax.rem(112 - e + L, L), 1)
                out = jnp.concatenate([out[:, :L], jnp.where(lane == 112, column, out[:, L:])], axis=1)
                x0[q * 8 + octant] = out.astype(BF)

    def outside(k, q):
        axis, shift = (k - 1) // 2, -1 if k % 2 else 1
        ghost = ghosts[k]
        for octant in range(8):
            if bits(octant)[axis] != (0 if shift < 0 else 1):
                continue
            x, y, oz = where_is(q, octant)
            c = oz * 16 + x * 4 + y
            if axis == 2:
                idx = x * 4 + y
                out = product(c, ghost[idx], ghost[16], idx)
                edge = 0 if shift < 0 else 15
                absent = scal[2] * 4 + scal[6] == edge
            else:
                along, other = (x, y) if axis == 0 else (y, x)
                spot = along + shift
                off = (spot < 0) | (spot > 3)
                spot = lax.rem(spot + 4, 4)
                idx = spot * 4 + other if axis == 0 else other * 4 + spot
                plane_main = jnp.where(off, ghost[oz * 4 + other], pz[oz][idx])
                plane_rest = jnp.where(off, ghost[8 + oz], pz[oz][16])
                out = product(c, plane_main, plane_rest, idx)
                edge = 0 if shift < 0 else (1, 3)[axis]
                absent = off & (scal[(3, 5)[axis]] == edge)
            xs[q * 8 + octant] = (out * jnp.where(absent, 0.0, 1.0)).astype(BF)

    def gather(ref, q, octants):
        acc = None
        for octant in octants:
            x, y, oz = where_is(q, octant)
            part = jnp.dot(pt[oz * 16 + x * 4 + y], ref[q * 8 + octant], preferred_element_type=F32)
            acc = part if acc is None else acc + part
        return acc

    def fold(raw, spots, slot):
        total = None
        for spot in spots:
            turned = pltpu.roll(raw, lax.rem(R * slot - R * spot + 2 * L, L), 1)
            total = turned if total is None else total + turned
        good = (lane >= R * slot) & (lane < R * slot + R)
        return jnp.where(good, total, 0.0)

    def finish_sides(axis, q):
        ax, ay = q // 2, lax.rem(q, 2)
        at = meta[E + q]
        remainder = (rem_out if axis == 1 else rem_in)[at]
        for side in range(2):
            acc = gather(xs, q, [o for o in range(8) if bits(o)[axis] == side])
            rows[at, 2 * (axis % 2) + side] = acc[:, :L].astype(BF)
            if axis == 0:
                nx = lax.rem(2 * ax + (-1 if side == 0 else 2) + 4, 4)
                spots = [nx * 4 + 2 * ay + v for v in range(2)]
            elif axis == 1:
                ny = lax.rem(2 * ay + (-1 if side == 0 else 2) + 4, 4)
                spots = [(2 * ax + v) * 4 + ny for v in range(2)]
            else:
                spots = [(2 * ax + v // 2) * 4 + 2 * ay + v % 2 for v in range(4)]
            remainder = remainder + fold(acc[:, L:], spots, 1 + 2 * axis + side)
        if axis == 2:
            rows[at, 2] = remainder.astype(BF)
        else:
            rem_out[at] = remainder

    def finish_centre(q):
        ax, ay = q // 2, lax.rem(q, 2)
        at = meta[E + q]
        acc = gather(x0, q, range(8))
        rows[at, 0] = acc[:, :L].astype(BF)
        raw = acc[:, L:]
        spots = [(2 * ax + v // 2) * 4 + 2 * ay + v % 2 for v in range(4)]
        moved = pltpu.roll(raw, 49 - 112 + L, 1)
        rem_out[at] = jnp.where(lane == 49, moved, fold(raw, spots, 0))

    for i, (k, outer) in enumerate(kinds):
        jac_copy(i).wait()
        spread(lambda row, i=i: jbuf[i % DEPTH, row], main, rest)
        if i + DEPTH < len(kinds):
            jac_copy(i + DEPTH).start()
        if i == 0:
            for copy in early_copies:
                copy.wait()
        if i == 1:
            for copy in late_copies:
                copy.wait()
            if res is not None:
                values = res[...].astype(F32)
                tail = jnp.concatenate([values[:, L:], jnp.zeros((E, L - R), F32)], axis=1)
                res_t[0:L, 0:E] = values[:, :L].T
                res_t[L:H, 0:E] = tail.T[: H - L]

        def run(q, carry, k=k, outer=outer):
            if k == 0:
                direct(q)
            elif outer:
                outside(k, q)
            else:
                same(k, q)
            if outer and k % 2 == 0:
                finish_sides((k - 1) // 2, q)
            if k == 6 and not outer:
                finish_centre(q)
            return carry

        lax.fori_loop(0, 4, run, 0)
    copies = [pltpu.make_async_copy(rows, rows_out, out_sems.at[0])]
    if rem_out is not None:
        copies.append(pltpu.make_async_copy(rem_out, rem_to, out_sems.at[1]))
    for copy in copies:
        copy.start()
    for copy in copies:
        copy.wait()


COMMON = [
    pltpu.VMEM((DEPTH, W, E, W), BF),
    pltpu.VMEM((H * PE, L), F32),
    pltpu.VMEM((H * PE, L), F32),
    pltpu.SemaphoreType.DMA((DEPTH,)),
    pltpu.SemaphoreType.DMA((6,)),
    pltpu.SemaphoreType.DMA((6,)),
    pltpu.SemaphoreType.DMA((2,)),
]
HALF = pltpu.VMEM((E, H, 2 * L), BF)
FULL = pltpu.VMEM((E, H, 2 * L), F32)
REM = pltpu.VMEM((4, H, L), F32)
REST = pltpu.HBM((4, H, L), F32)


def centre_kernel(scal, meta, jac, pz0, pz1, pt, res, rows_out, rem_to, *scratch):
    jbuf, main, rest, j_sems, e_sems, l_sems, o_sems, x0, keep, vz0, vz1, vpt, vres, res_t, rows, rem_out = scratch
    block_kernel(
        [(k, False) for k in range(7)], scal, meta, jac,
        [(pz0, vz0), (pz1, vz1)], [(pt, vpt), (res, vres)],
        ((vz0, vz1), {}, vpt, (vres, res_t), None),
        rows, rows_out.at[:, pl.ds(4, 1)], rem_out, rem_to,
        (jbuf, main, rest, x0, None, keep, j_sems, e_sems, l_sems, o_sems),
    )


def sides_kernel(scal, meta, jac, pz0, pz1, pt, gx, gym, gyp, rem_in, started, rows_out, rem_to, *scratch):
    jbuf, main, rest, j_sems, e_sems, l_sems, o_sems = scratch[:7]
    xs, vz0, vz1, vpt, vx, vym, vyp, vrem, rows, rem_out = scratch[7:]
    block_kernel(
        [(k, True) for k in range(1, 5)], scal, meta, jac,
        [(pz0, vz0), (pz1, vz1), (gx, vx)], [(pt, vpt), (rem_in, vrem), (gym, vym), (gyp, vyp)],
        ((vz0, vz1), {1: vx, 2: vx, 3: vym, 4: vyp}, vpt, (None, None), vrem),
        rows, rows_out.at[:, pl.ds(0, 4)], rem_out, rem_to,
        (jbuf, main, rest, None, xs, None, j_sems, e_sems, l_sems, o_sems),
    )


def depth_kernel(scal, meta, jac, pt, gzm, gzp, rem_in, rows_out, *scratch):
    jbuf, main, rest, j_sems, e_sems, l_sems, o_sems, xs, vpt, vzm, vzp, vrem, rows = scratch
    block_kernel(
        [(k, True) for k in (5, 6)], scal, meta, jac,
        [(gzm, vzm)], [(pt, vpt), (gzp, vzp), (rem_in, vrem)],
        (None, {5: vzm, 6: vzp}, vpt, (None, None), vrem),
        rows, rows_out, None, None,
        (jbuf, main, rest, None, xs, None, j_sems, e_sems, l_sems, o_sems),
    )


def block_call(kernel, operands, out_shape, scratch, name, aliases, cost):
    return pl.pallas_call(
        kernel,
        in_specs=[smem(), smem()] + [anywhere()] * (len(operands) - 2),
        out_specs=[anywhere()] * len(out_shape),
        out_shape=out_shape,
        scratch_shapes=COMMON + scratch,
        input_output_aliases=aliases,
        compiler_params=pltpu.CompilerParams(vmem_limit_bytes=VMEM_LIMIT),
        cost_estimate=pl.CostEstimate(flops=cost, bytes_accessed=1_000_000, transcendentals=0),
        name=name,
    )(*operands)


def final_kernel(scal, *refs):
    held = refs[:10]
    coarse, restricted, out, s1, s2, out_sems = refs[10:]
    lane = lax.broadcasted_iota(jnp.int32, (H, L), 1)

    def plane_of(n, slot):
        part, plane = (0, n) if n < 5 else (1, n - 5)
        z, y = slot // 4, slot % 4
        which, row = [(0, z), (1, z), (3 + z // 2, z % 2), (2, z)][y]
        return held[5 * part + which][row, plane].astype(F32)

    def out_copy(k):
        return pltpu.make_async_copy(out.at[k % 3], coarse.at[k], out_sems.at[k])

    @pl.when(scal[4] == 0)
    def _():
        out[0] = jnp.zeros((W, 16, W), BF)
        restricted[...] = jnp.zeros_like(restricted)
        zero_copies = [pltpu.make_async_copy(out.at[0], coarse.at[k], out_sems.at[k]) for k in range(7)]
        for copy in zero_copies:
            copy.start()
        for copy in zero_copies:
            copy.wait()

    @pl.when(scal[4] == 1)
    def _():
        for k in range(7):
            for slot in range(16):
                s1[pl.ds(slot, H, stride=PS), :] = plane_of([4, 0, 1, 2, 3, 5, 6][k], slot)
                tail = plane_of(7, slot)
                s2[pl.ds(slot, H, stride=PS), :] = pltpu.roll(tail, L - R * k, 1) if k else tail
            if k >= 3:
                out_copy(k - 3).wait()

            def write(i, carry, k=k):
                for u in range(27):
                    row = i * 27 + u
                    at = pl.ds(row * PS, 16)
                    out[k % 3, row] = jnp.concatenate([s1[at, :], s2[at, :R]], axis=1).astype(BF)
                return carry

            lax.fori_loop(0, W // 27, write, 0)
            out_copy(k).start()
        acc = jnp.zeros((H, L), F32)
        for slot in range(16):
            turned = pltpu.roll(plane_of(7, slot), (slot - 49 + L) % L, 1)
            acc = jnp.where(lane == slot, turned, acc)
        restricted[...] = acc.T[:16, :W].astype(BF)
        for k in range(4, 7):
            out_copy(k).wait()


def final_call(scal, rows):
    rows = [pltpu.with_memory_space_constraint(a, pltpu.VMEM) for a in rows]
    return pl.pallas_call(
        final_kernel,
        in_specs=[smem()] + [vmem()] * 10,
        out_specs=[anywhere(), vmem()],
        out_shape=[jax.ShapeDtypeStruct((7, W, 16, W), BF), jax.ShapeDtypeStruct((16, W), BF)],
        scratch_shapes=[
            pltpu.VMEM((3, W, 16, W), BF),
            pltpu.VMEM((H * PS, L), F32),
            pltpu.VMEM((H * PS, L), F32),
            pltpu.SemaphoreType.DMA((7,)),
        ],
        compiler_params=pltpu.CompilerParams(vmem_limit_bytes=VMEM_LIMIT),
        name="assemble",
    )(scal, *rows)


DOWN = [(1, 0), (2, 1), (3, 2), (0, 3)]
UP = [(3, 0), (0, 1), (1, 2), (2, 3)]


def to_owner_row(rows):
    return lax.all_to_all(rows, "zz", split_axis=0, concat_axis=0, tiled=True)


def along_ring(held):
    down = lax.ppermute(held, "yy", DOWN)
    up = lax.ppermute(held, "yy", UP)
    return down, up


def forward(down, up):
    return lax.ppermute(down[:2], "yy", [(1, 0)]), lax.ppermute(up[2:], "yy", [(3, 0)])


def body(jacobian, prolong, residual, neighbours, agg_map, owners):
    gx, gy = lax.axis_index("gx"), lax.axis_index("gy")
    zz, yy = lax.axis_index("zz"), lax.axis_index("yy")
    device = (gx * 4 + gy) * 16 + zz * 4 + yy
    scal = jnp.stack(
        [device * E, device * 4, zz, gx, (yy == 0).astype(jnp.int32), gy, yy]
    ).astype(jnp.int32)
    jac = jnp.transpose(jacobian, (1, 2, 0, 3))
    pro = jnp.transpose(prolong, (1, 0, 2))
    meta, pz0, pz1, xs, ys0, ys1, pt = pack_call(
        scal, stay(neighbours.T), stay(agg_map), stay(owners), stay(pro)
    )
    gz = ("zz", "yy")
    ghost_x = lax.ppermute(xs, "gx", [(0, 1), (1, 0)])
    ghost_zm = lax.ppermute(pz1, gz, [(i, (i + 1) % 16) for i in range(16)])
    ghost_zp = lax.ppermute(pz0, gz, [((i + 1) % 16, i) for i in range(16)])
    ghost_ym = lax.ppermute(ys1, "gy", [(i, (i + 1) % 4) for i in range(4)])
    ghost_yp = lax.ppermute(ys0, "gy", [((i + 1) % 4, i) for i in range(4)])
    five = jax.ShapeDtypeStruct((4, 5, H, L), BF)
    z_face, side_face = [pltpu.VMEM((n, H, L), BF) for n in (17, 10)]
    turned = pltpu.VMEM((E, H, H), BF)
    first, rem = block_call(
        centre_kernel, (scal, meta, jac, pz0, pz1, pt, stay(residual)), [five, REST],
        [HALF, FULL, z_face, z_face, turned, pltpu.VMEM((E, W), BF), pltpu.VMEM((H, L), F32), pltpu.VMEM((4, 1, H, L), BF), REM],
        "centre", {}, 18_000_000_000,
    )
    first, rem = block_call(
        sides_kernel, (scal, meta, jac, pz0, pz1, pt, ghost_x, ghost_ym, ghost_yp, stay(rem), first), [five, REST],
        [HALF, z_face, z_face, turned, side_face, side_face, side_face, REM, pltpu.VMEM((4, 4, H, L), BF), REM],
        "sides", {10: 0}, 12_000_000_000,
    )
    held1 = to_owner_row(first)
    (second,) = block_call(
        depth_kernel, (scal, meta, jac, pt, ghost_zm, ghost_zp, stay(rem)),
        [jax.ShapeDtypeStruct((4, 3, H, L), BF)],
        [HALF, turned, z_face, z_face, REM, pltpu.VMEM((4, 3, H, L), BF)],
        "depth", {}, 9_000_000_000,
    )
    held1, second = lax.optimization_barrier((held1, second))
    down1, up1 = along_ring(held1)
    held2 = to_owner_row(second)
    twice1 = forward(down1, up1)
    down2, up2 = along_ring(held2)
    twice2 = forward(down2, up2)
    coarse, restricted = final_call(scal, (held1, down1, up1) + twice1 + (held2, down2, up2) + twice2)
    return jnp.transpose(coarse, (2, 0, 1, 3)), restricted


def solution(mesh):
    fine = Mesh(mesh.devices.reshape(2, 4, 4, 4), ("gx", "gy", "zz", "yy"))
    every = ("gx", "gy", "zz", "yy")
    return jax.shard_map(
        body,
        mesh=fine,
        in_specs=(P(every), P(every), P(every), P(every), P(every), P(every)),
        out_specs=(P(every), P(every)),
        check_vma=False,
    )
```
